32 devices in a mesh: tm: 8 (over z, x), sensor: 4 (over y, core).
Axes of the slice: x: 2, y: 2, z: 4, core: 2. Of those that a mesh axis runs over, the one named last changes fastest.
Arguments:
- state_tiles: bfloat16 [8192, 4096], P('sensor', 'tm'), may hold values from -6 to 6
- sketch: bfloat16 [1024, 128], replicated, may hold values from -0.1875 to 0.1875
- probe_cell: int32 [4, 4, 128], P('sensor'), may hold values from 0 to 2047
- probe_row: int32 [4, 4, 128], P('sensor'), may hold values from -1 to 255, as said below
Outputs:
- hankel_sketch: float32 [256, 1024, 128], P('tm', 'sensor')
- column_image: float32 [1024, 128], P(('tm', 'sensor'))
The draws below stay inside these ranges and needn't reach their ends.
Inputs may be any that keep to these rules, and one draw needn't show every extreme that they name: `probe_row`: every sensor row of every owner is filled by exactly one slot over all tiles; for each owner, the tiles that feed it fill all 128 of their slots to it and the other tiles none, and exactly half of the tiles feed each owner.
All inputs are finite; a program needn't handle non-finite values.
Results may differ from the reference program's by a relative error of at most 0.0003.
Values may be sent and summed in bfloat16 or wider, within the bound.
No kernel may reach another device: no remote copies, remote signals or barrier semaphores. Data moves between devices by JAX's collectives and lax.ppermute only.
A program may use at most 64 MiB of HBM per device.

```python
import math
import jax
import jax.numpy as jnp
from jax import lax

INPUTS = 16
SENS_DEV = 256
SK = 128
CELLS_DEV = 2048
SENSORS = 1024
STEPS = 256
KC = 64
CELLS = 8192
TILES = 4
CAPD = 128
N_SENSOR = 4


def draw_probe_row(key, part):
    key_bias, key_jitter, key_shuffle = jax.random.split(jax.random.fold_in(key, 7), 3)
    heaviness = jax.random.randint(key_bias, (TILES,), 0, 4)
    jitter = jax.random.randint(key_jitter, (TILES, TILES), 0, 6)
    scores = (heaviness[None, :] * 6 + jitter) * TILES + jnp.arange(TILES, dtype=jnp.int32)[None, :]
    ranking = jnp.argsort(-scores, axis=1, stable=True)
    tile_rank = jnp.argsort(ranking, axis=1, stable=True).astype(jnp.int32)
    shuffled = jax.vmap(lambda k: jax.random.permutation(k, SENS_DEV))(jax.random.split(key_shuffle, TILES)).astype(jnp.int32)
    slot_ids = jnp.arange(CAPD, dtype=jnp.int32)
    position = jnp.minimum(tile_rank[:, :, None], TILES // 2 - 1) * CAPD + slot_ids[None, None, :]
    picked = jnp.take_along_axis(shuffled, position.reshape(TILES, TILES * CAPD), axis=1).reshape(TILES, TILES, CAPD)
    return jnp.where(tile_rank[:, :, None] < TILES // 2, picked, -1).astype(jnp.int32)


def set_ends(entries, own_key, smallest, largest):
    extent = entries.shape
    place = [jax.random.randint(jax.random.fold_in(own_key, axis), (), 0, extent[axis]) for axis in range(len(extent))]
    entries = entries.at[tuple(place)].set(smallest)
    longest = extent.index(max(extent))
    place[longest] = (place[longest] + 1) % extent[longest]
    return entries.at[tuple(place)].set(largest)


def block_scale(rng, dims, cuts, least, largest):
    level = 1.0
    for dim, parts in cuts:
        steps = jax.random.uniform(jax.random.fold_in(jax.random.fold_in(rng, 6), dim), (parts,), jnp.float32, least / len(cuts), largest / len(cuts))
        level = level * jnp.repeat(jnp.exp(steps), dims[dim] // parts).reshape((-1,) + (1,) * (len(dims) - 1 - dim))
    return level


def gaussian(rng, shape, deviation, bound, pieces=(), kind=jnp.bfloat16):
    level = block_scale(rng, shape, pieces, -0.22, 0.18) if pieces else 1.0
    result = jax.random.normal(rng, shape, jnp.float32) * deviation * level
    return jnp.minimum(jnp.maximum(result, -bound), bound).astype(kind)


def setup_inputs(seed: int = 0) -> dict:
    splits = jax.random.split(jax.random.key(seed), 5)
    state_tiles = gaussian(splits[0], (CELLS, STEPS * INPUTS), 1.0, 6.0, ((0, 4), (1, 8)))
    sketch = gaussian(splits[1], (KC * INPUTS, SK), (KC * INPUTS) ** -0.5, 0.1875)
    probe_cell = set_ends(jax.random.randint(splits[2], (N_SENSOR, N_SENSOR, CAPD), 0, CELLS_DEV), jax.random.fold_in(splits[2], 1), 0, CELLS_DEV - 1).astype(jnp.int32)
    probe_row = draw_probe_row(jax.random.fold_in(splits[4], 71), 0)
    return {"state_tiles": state_tiles, "sketch": sketch, "probe_cell": probe_cell, "probe_row": probe_row}


def reference(state_tiles, sketch, probe_cell, probe_row):
    tile_ids = jnp.arange(N_SENSOR, dtype=jnp.int32)
    source = (tile_ids[:, None, None] * CELLS_DEV + probe_cell).reshape(-1)
    rows_tile = jnp.transpose(probe_row, (1, 0, 2))
    target = jnp.where(rows_tile >= 0, tile_ids[None, :, None] * SENS_DEV + rows_tile, SENSORS).reshape(-1)
    outputs = jnp.zeros((SENSORS, STEPS * INPUTS), jnp.bfloat16).at[target].set(state_tiles[source], mode='drop')
    padded = jnp.concatenate([outputs, jnp.zeros((SENSORS, KC * INPUTS), jnp.bfloat16)], axis=1)
    group_size = math.gcd(STEPS, 8)
    sketch_wide = sketch.astype(jnp.float32)

    def one_block(total, block):
        starts = block * group_size + jnp.arange(group_size, dtype=jnp.int32)
        windows = jax.vmap(lambda first: lax.dynamic_slice_in_dim(padded, first * INPUTS, KC * INPUTS, 1))(starts)
        windows = windows.astype(jnp.float32)
        image = jnp.einsum('isk,kc->isc', windows, sketch_wide)
        image_bf = lax.optimization_barrier(image.astype(jnp.bfloat16)).astype(jnp.float32)
        total = total + jnp.einsum('isk,isc->kc', windows, image_bf)
        return (total, image)
    total, images = lax.scan(one_block, jnp.zeros((KC * INPUTS, SK), jnp.float32), jnp.arange(STEPS // group_size, dtype=jnp.int32))
    hankel_sketch = images.reshape(STEPS, SENSORS, SK)
    column_image = total * (1.0 / math.sqrt(SENSORS * STEPS))
    return (hankel_sketch, column_image)
```

```python
import math

import jax
import jax.numpy as jnp
from jax import lax
from jax.experimental import pallas as pl
from jax.experimental.pallas import tpu as pltpu
from jax.sharding import PartitionSpec as P

INPUTS = 16
SENS_DEV = 256
LANES = 128


def shifted(x, axis, by):
    count = lax.axis_size(axis)
    pairs = [(i, i + by) for i in range(count) if 0 <= i + by < count]
    return lax.ppermute(x, axis, pairs)


def crossed(x, axes, mask):
    count = math.prod(lax.axis_size(a) for a in axes)
    return lax.ppermute(x, axes, [(i, i ^ mask) for i in range(count)])


def exchange(parts, axis):
    count = lax.axis_size(axis)
    me = lax.axis_index(axis)
    got = [lax.dynamic_index_in_dim(parts, me, 0, keepdims=False)]
    for mask in range(1, count):
        got.append(crossed(lax.dynamic_index_in_dim(parts, me ^ mask, 0, keepdims=False), (axis,), mask))
    return got


def reduce_scatter(total, axes, rounds):
    count = math.prod(lax.axis_size(a) for a in axes)
    me = jnp.int32(0)
    for a in axes:
        me = me * lax.axis_size(a) + lax.axis_index(a)
    bits = int(math.log2(count))
    value = total.reshape((2,) * bits + (total.shape[0] // count, total.shape[1]))
    left = list(range(bits))
    for bunch in rounds:
        dims = [left.index(b) for b in bunch]
        value = jnp.moveaxis(value, dims, range(len(bunch)))
        rest = value.shape[len(bunch):]
        value = value.reshape((2 ** len(bunch),) + rest)
        mine = jnp.int32(0)
        for b in bunch:
            mine = mine * 2 + ((me >> (bits - 1 - b)) & 1)
        acc = lax.dynamic_index_in_dim(value, mine, 0, keepdims=False)
        for mask in range(1, 2 ** len(bunch)):
            flip = 0
            for place, b in enumerate(bunch):
                if (mask >> (len(bunch) - 1 - place)) & 1:
                    flip |= 1 << (bits - 1 - b)
            acc = acc + crossed(lax.dynamic_index_in_dim(value, mine ^ mask, 0, keepdims=False), axes, flip)
        value = acc
        for b in bunch:
            left.remove(b)
    return value


def products(blocks, wide, span, scale):
    rows, width = blocks[0].shape
    columns = wide.shape[1] // (LANES // INPUTS)
    group = LANES // INPUTS
    groups = width // LANES
    reach = wide.shape[0]
    n_blocks = len(blocks)

    def kernel(*refs):
        block_refs = refs[:n_blocks]
        wide_ref, out_ref, image_ref, ext, turned, rounded = refs[n_blocks:]
        g = pl.program_id(0)

        @pl.when(g == 0)
        def _():
            for b in range(n_blocks):
                ext[:, b * width : (b + 1) * width] = block_refs[b][...]

        window = ext[:, pl.ds(pl.multiple_of(g * LANES, LANES), reach)]
        image = jnp.dot(window, wide_ref[...], preferred_element_type=jnp.float32)
        at = pl.ds(pl.multiple_of(g * rows, rows), rows)
        rounded[at, :] = image.astype(jnp.bfloat16)
        for o in range(group):
            out_ref[o] = image[:, o * columns : (o + 1) * columns]
        turned[:, at] = window.T

        @pl.when(g == groups - 1)
        def _():
            image_ref[...] = jnp.zeros_like(image_ref)

            def pair(p, carry):
                first = pl.multiple_of(p * 2 * INPUTS, 2 * INPUTS)
                part = jnp.dot(
                    turned[pl.ds(first, span + INPUTS), :],
                    rounded[:, pl.ds(pl.multiple_of(p * 2 * columns, 2 * columns), 2 * columns)],
                    preferred_element_type=jnp.float32,
                )
                image_ref[...] += part[:span, :columns] + part[INPUTS:, columns:]
                return carry

            lax.fori_loop(0, group // 2, pair, 0)
            image_ref[...] *= scale

    return pl.pallas_call(
        kernel,
        grid=(groups,),
        in_specs=[pl.BlockSpec((rows, width), lambda g: (0, 0))] * n_blocks
        + [pl.BlockSpec(wide.shape, lambda g: (0, 0))],
        out_specs=[
            pl.BlockSpec((group, rows, columns), lambda g: (g, 0, 0)),
            pl.BlockSpec((span, columns), lambda g: (0, 0)),
        ],
        out_shape=[
            jax.ShapeDtypeStruct((groups * group, rows, columns), jnp.float32),
            jax.ShapeDtypeStruct((span, columns), jnp.float32),
        ],
        scratch_shapes=[
            pltpu.VMEM((rows, n_blocks * width), jnp.bfloat16),
            pltpu.VMEM((reach, groups * rows), jnp.bfloat16),
            pltpu.VMEM((groups * rows, group * columns), jnp.bfloat16),
        ],
        compiler_params=pltpu.CompilerParams(vmem_limit_bytes=48 * 1024 * 1024),
    )(*blocks, wide)


def local(state_tiles, sketch, probe_cell, probe_row):
    n_tiles = lax.axis_size("sensor")
    cells_here, width = state_tiles.shape
    steps_here = width // INPUTS
    capacity = probe_cell.shape[2]
    span, columns = sketch.shape
    cell_index = probe_cell[0].reshape(-1)
    onehot = (cell_index[:, None] == jnp.arange(cells_here, dtype=jnp.int32)[None, :]).astype(
        jnp.bfloat16
    )
    picked = jnp.dot(onehot, state_tiles, preferred_element_type=jnp.float32).astype(jnp.bfloat16)
    arrived = exchange(picked.reshape(n_tiles, capacity, width), "sensor")
    me = lax.axis_index("sensor")
    own_block = 0
    for mask in range(n_tiles):
        row_index = lax.dynamic_index_in_dim(probe_row[0], me ^ mask, 0, keepdims=False)
        placement = (row_index[None, :] == jnp.arange(SENS_DEV, dtype=jnp.int32)[:, None]).astype(
            jnp.bfloat16
        )
        own_block = own_block + jnp.dot(placement, arrived[mask], preferred_element_type=jnp.float32)
    own_block = own_block.astype(jnp.bfloat16)
    halos = -(-(span // INPUTS - 1) // steps_here)
    blocks = [own_block] + [shifted(own_block, "tm", -k) for k in range(1, halos + 1)]
    group = LANES // INPUTS
    wide = jnp.stack(
        [jnp.pad(sketch, ((o * INPUTS, LANES - o * INPUTS), (0, 0))) for o in range(group)], axis=1
    ).reshape(span + LANES, group * columns)
    scale = 1.0 / math.sqrt(SENS_DEV * n_tiles * steps_here * lax.axis_size("tm"))
    hankel_sketch, total = products(blocks, wide, span, scale)
    tm_bits = int(math.log2(lax.axis_size("tm")))
    sensor_bits = int(math.log2(n_tiles))
    last = tm_bits + sensor_bits - 1
    rounds = [[last], list(range(tm_bits - 1, last)), list(range(tm_bits - 1))]
    column_image = reduce_scatter(total, ("tm", "sensor"), rounds)
    return (hankel_sketch, column_image)


def solution(mesh):
    placed = (P("sensor", "tm"), P(), P("sensor", None, None), P("sensor", None, None))
    return jax.shard_map(
        local,
        mesh=mesh,
        in_specs=placed,
        out_specs=(P("tm", "sensor", None), P(("tm", "sensor"), None)),
        check_vma=False,
    )
```

```python
import math

import jax
import jax.numpy as jnp
from jax import lax
from jax.experimental import pallas as pl
from jax.experimental.pallas import tpu as pltpu
from jax.sharding import PartitionSpec as P

INPUTS = 16
SENS_DEV = 256
LANES = 128
TAIL = 16
MIB = 1024 * 1024
F32 = jnp.float32
BF16 = jnp.bfloat16


def shifted(x, axis, by):
    count = lax.axis_size(axis)
    pairs = [(i, i + by) for i in range(count) if 0 <= i + by < count]
    return lax.ppermute(x, axis, pairs)


def crossed(x, axes, mask):
    count = math.prod(lax.axis_size(a) for a in axes)
    return lax.ppermute(x, axes, [(i, i ^ mask) for i in range(count)])


def pick_rows(state_tiles, probe_cell, probe_row):
    cells_here, width = state_tiles.shape
    tiles, capacity = probe_cell.shape
    rows = tiles * capacity
    half = rows // 2
    steps = 4
    chunk = cells_here // steps

    def kernel(cell_ref, row_ref, state_ref, *refs):
        parts = refs[:tiles]
        first, second, swap, slot, total = refs[tiles:]
        k = pl.program_id(0)
        me = lax.axis_index("sensor")

        @pl.when(k == 0)
        def _():
            for m in range(tiles):
                line = cell_ref[pl.ds(me ^ m, 1), :]
                slot[m * capacity : (m + 1) * capacity, :] = jnp.broadcast_to(line, (LANES, capacity)).T
            total[...] = jnp.zeros_like(total)

        lane = lax.broadcasted_iota(jnp.int32, (rows, LANES), 1) + k * chunk
        wanted = slot[...]
        chosen = jnp.concatenate(
            [jnp.where(wanted == lane + c, 1.0, 0.0).astype(BF16) for c in range(0, chunk, LANES)], axis=1
        )
        total[...] += jnp.dot(chosen, state_ref[...], preferred_element_type=F32)

        @pl.when(k == steps - 1)
        def _():
            odd = lax.rem(lax.axis_index("tm"), 2)
            got = total[...].astype(BF16)
            first[...] = got[:half]
            second[...] = got[half:]

            @pl.when(odd == 0)
            def _():
                swap[...] = got[:half]

            @pl.when(odd == 1)
            def _():
                swap[...] = got[half:]

            for m in range(tiles):
                parts[m][:capacity, :] = got[m * capacity : (m + 1) * capacity]
                filled = jnp.broadcast_to(row_ref[pl.ds(me ^ m, 1), :1], (TAIL, width)) >= 0
                parts[m][capacity:, :] = jnp.where(filled, 1.0, 0.0).astype(BF16)

    whole = lambda shape: pl.BlockSpec(shape, lambda k: (0,) * len(shape))
    shapes = [(capacity + TAIL, width)] * tiles + [(half, width)] * 3
    return pl.pallas_call(
        kernel,
        grid=(steps,),
        in_specs=[whole(probe_cell.shape), whole(probe_row.shape), pl.BlockSpec((chunk, width), lambda k: (k, 0))],
        out_specs=[whole(s) for s in shapes],
        out_shape=[jax.ShapeDtypeStruct(s, BF16) for s in shapes],
        scratch_shapes=[pltpu.VMEM((rows, LANES), jnp.int32), pltpu.VMEM((rows, width), F32)],
        compiler_params=pltpu.CompilerParams(vmem_limit_bytes=24 * MIB),
    )(probe_cell, probe_row, state_tiles)


def place_rows(probe_row, parts):
    tiles, capacity = probe_row.shape
    width = parts[0].shape[1]

    def kernel(row_ref, *refs):
        out_ref = refs[tiles]
        me = lax.axis_index("sensor")
        sensor = lax.broadcasted_iota(jnp.int32, (SENS_DEV, capacity), 0)
        total = jnp.zeros((SENS_DEV, width), F32)
        for m in range(tiles):
            chosen = jnp.where(row_ref[pl.ds(me ^ m, 1), :] == sensor, 1.0, 0.0).astype(BF16)
            total += jnp.dot(chosen, refs[m][:capacity, :], preferred_element_type=F32)
        out_ref[...] = total.astype(BF16)

    return pl.pallas_call(
        kernel,
        out_shape=jax.ShapeDtypeStruct((SENS_DEV, width), BF16),
        compiler_params=pltpu.CompilerParams(vmem_limit_bytes=16 * MIB),
    )(probe_row, *parts)


def widen(sketch):
    span, columns = sketch.shape
    group = LANES // INPUTS

    def kernel(sketch_ref, out_ref):
        out_ref[...] = jnp.zeros_like(out_ref)
        for o in range(group):
            out_ref[o * INPUTS : o * INPUTS + span, o * columns : (o + 1) * columns] = sketch_ref[...]

    return pl.pallas_call(
        kernel,
        out_shape=jax.ShapeDtypeStruct((span + LANES, group * columns), BF16),
        compiler_params=pltpu.CompilerParams(vmem_limit_bytes=16 * MIB),
    )(sketch)


def hankel_times(blocks, wide):
    rows, width = blocks[0].shape
    group = LANES // INPUTS
    columns = wide.shape[1] // group
    groups = width // LANES
    reach = wide.shape[0]
    n_blocks = len(blocks)

    def kernel(*refs):
        wide_ref, out_ref, ext = refs[n_blocks:]
        g = pl.program_id(0)

        @pl.when(g == 0)
        def _():
            for b in range(n_blocks):
                ext[:, b * width : (b + 1) * width] = refs[b][...]

        window = ext[:, pl.ds(pl.multiple_of(g * LANES, LANES), reach)]
        image = jnp.dot(window, wide_ref[...], preferred_element_type=F32)
        for o in range(group):
            out_ref[o] = image[:, o * columns : (o + 1) * columns]

    return pl.pallas_call(
        kernel,
        grid=(groups,),
        in_specs=[pl.BlockSpec((rows, width), lambda g: (0, 0))] * n_blocks
        + [pl.BlockSpec(wide.shape, lambda g: (0, 0))],
        out_specs=pl.BlockSpec((group, rows, columns), lambda g: (g, 0, 0)),
        out_shape=jax.ShapeDtypeStruct((groups * group, rows, columns), F32),
        scratch_shapes=[pltpu.VMEM((rows, n_blocks * width), BF16)],
        compiler_params=pltpu.CompilerParams(vmem_limit_bytes=20 * MIB),
    )(*blocks, wide)


def across(a, b):
    return lax.dot_general(a, b, (((0,), (0,)), ((), ())), preferred_element_type=F32)


def gram_image(place, first, second, back, ahead, swap, parts, sketch, scale):
    half, width = first.shape
    span, columns = sketch.shape
    tiles = len(parts)
    capacity = 2 * half // tiles
    group = LANES // INPUTS
    pair = 2 * LANES
    groups = span // LANES

    def kernel(place_ref, first_ref, second_ref, back_ref, ahead_ref, swap_ref, *refs):
        part_refs = refs[:tiles]
        sketch_ref, image_ref, own, left, right, lag, early, full, turned = refs[tiles:]
        spot = place_ref[0]
        odd = lax.rem(spot, 2)
        for m in range(tiles):
            at = slice(m * capacity, (m + 1) * capacity)
            source, base = (first_ref, 0) if m < tiles // 2 else (second_ref, half)
            keep = part_refs[m][capacity : capacity + TAIL, :][:1]
            own[at, :] = source[m * capacity - base : (m + 1) * capacity - base, :] * keep

        @pl.when(odd == 0)
        def _():
            for m in range(tiles // 2, tiles):
                at = slice(m * capacity - half, (m + 1) * capacity - half)
                keep = part_refs[m][capacity : capacity + TAIL, :][:1]
                mine = swap_ref[at, :] * keep
                right[at, :] = mine
                left[half + m * capacity - half : half + (m + 1) * capacity - half, :] = mine
            left[:half, :] = own[half:, :]
            right[half : 2 * half, :] = ahead_ref[...]

        @pl.when(odd == 1)
        def _():
            for m in range(tiles // 2):
                at = slice(m * capacity, (m + 1) * capacity)
                keep = part_refs[m][capacity : capacity + TAIL, :][:1]
                mine = swap_ref[at, :] * keep
                left[at, :] = mine
                right[half + m * capacity : half + (m + 1) * capacity, :] = mine
            right[:half, :] = own[:half, :]
            left[half : 2 * half, :] = back_ref[...]

        left[2 * half : 3 * half, :] = back_ref[...]
        left[3 * half :, :] = own[half:, :]
        right[2 * half : 3 * half, :] = own[:half, :]
        right[3 * half :, :] = ahead_ref[...]
        lag[...] = jnp.zeros_like(lag)

        @pl.when(spot < 2)
        def _():
            early[...] = jnp.zeros_like(early)

        for q in range(width // pair):
            at = slice(q * pair, (q + 1) * pair)
            low = q * pair
            same = across(own[:, at], own[:, low:])
            n = width - low
            lag[:, :n] += same[:LANES]
            lag[:, : n - LANES] += same[LANES:, LANES:]
            near = across(left[:half, at], right[:half, :])
            one = near + across(left[half : 2 * half, at], right[half : 2 * half, :])
            lag[:, n : n + width] += one[:LANES]
            lag[:, n - LANES : n - LANES + width] += one[LANES:]
            two = across(left[2 * half :, at], right[2 * half :, : low + pair])
            lag[:, n + width :] += two[:LANES, : low + LANES]
            lag[:, n + width - LANES :] += two[LANES:, :]

            @pl.when(spot == 0)
            def _():
                early[at, low:width] = same
                early[at, width : 2 * width] = near

            @pl.when(spot == 1)
            def _():
                early[width + low : width + low + pair, width + low : 2 * width] = same
                early[at, width : 2 * width] = near

        strip = lag[:INPUTS, :span]
        for o in range(1, group):
            strip += pltpu.roll(lag[o * INPUTS : (o + 1) * INPUTS, :], span + LANES - o * INPUTS, 1)[:, :span]
        lane = lax.broadcasted_iota(jnp.int32, strip.shape, 1)
        strip = jnp.where(lane < INPUTS, 0.5 * strip, strip)
        for o in range(group):
            moved = strip if o == 0 else jnp.where(lane < o * INPUTS, 0.0, pltpu.roll(strip, o * INPUTS, 1))
            lag[o * INPUTS : (o + 1) * INPUTS, :span] = moved
        for j in range(groups):
            full[j * LANES : (j + 1) * LANES, j * LANES :] = lag[:, : span - j * LANES]
            if j % 2:
                full[j * LANES : (j + 1) * LANES, (j - 1) * LANES : j * LANES] = jnp.zeros((LANES, LANES), F32)

        @pl.when(spot < 2)
        def _():
            r = lax.broadcasted_iota(jnp.int32, (LANES, LANES), 0) // INPUTS
            c = lax.broadcasted_iota(jnp.int32, (LANES, LANES), 1) // INPUTS
            weight = jnp.where(c > r, 1.0, jnp.where(c == r, 0.5, 0.0))
            for j in range(groups):
                at = slice(j * LANES, (j + 1) * LANES)
                early[at, at] = early[at, at] * weight
                full[at, at] += early[at, at]
                if j + 1 < groups:
                    rest = slice((j + 1) * LANES, span)
                    full[at, rest] += early[at, rest]
            by = 1
            while by < group:
                step = by * INPUTS
                for j in reversed(range(groups)):
                    at = slice(j * LANES, (j + 1) * LANES)
                    if j:
                        source = early[j * LANES - step : (j + 1) * LANES - step, (j - 1) * LANES :]
                        early[at, j * LANES :] += pltpu.roll(source, step, 1)[:, LANES:]
                    else:
                        source = early[: LANES - step, :]
                        early[step:LANES, :] += pltpu.roll(source, step, 1)
                by *= 2
            by = 1
            while by < groups:
                for j in reversed(range(by, groups)):
                    early[j * LANES : (j + 1) * LANES, j * LANES :] += early[
                        (j - by) * LANES : (j - by + 1) * LANES, (j - by) * LANES : span - by * LANES
                    ]
                by *= 2
            for j in range(groups):
                at = slice(j * LANES, (j + 1) * LANES)
                full[at, at] -= jnp.where(c >= r, early[at, at], 0.0)
                if j + 1 < groups:
                    rest = slice((j + 1) * LANES, span)
                    full[at, rest] -= early[at, rest]

        for q in range(span // pair):
            at = slice(q * pair, (q + 1) * pair)
            value = full[at, q * pair :]
            high = value.astype(BF16)
            low = (value - high.astype(F32)).astype(BF16)
            below = sketch_ref[q * pair :, :]
            image_ref[at, :] = jnp.dot(high, below, preferred_element_type=F32) + jnp.dot(
                low, below, preferred_element_type=F32
            )
            tall = sketch_ref[at, :]
            down = across(tall, high) + across(tall, low)
            if q == 0:
                turned[...] = down
            else:
                turned[:, q * pair :] += down
        image_ref[...] = (image_ref[...] + turned[...].T) * scale

    vmem = pl.BlockSpec(memory_space=pltpu.VMEM)
    smem = pl.BlockSpec(memory_space=pltpu.SMEM)
    return pl.pallas_call(
        kernel,
        in_specs=[smem] + [vmem] * (6 + tiles),
        out_specs=vmem,
        out_shape=jax.ShapeDtypeStruct((span, columns), F32),
        scratch_shapes=[
            pltpu.VMEM((2 * half, width), BF16),
            pltpu.VMEM((4 * half, width), BF16),
            pltpu.VMEM((4 * half, width), BF16),
            pltpu.VMEM((LANES, span + LANES), F32),
            pltpu.VMEM((span, span), F32),
            pltpu.VMEM((span, span), F32),
            pltpu.VMEM((columns, span), F32),
        ],
        compiler_params=pltpu.CompilerParams(vmem_limit_bytes=28 * MIB),
    )(place, first, second, back, ahead, swap, *parts, sketch)


def reduce_scatter(total, axes, rounds):
    count = math.prod(lax.axis_size(a) for a in axes)
    me = jnp.int32(0)
    for a in axes:
        me = me * lax.axis_size(a) + lax.axis_index(a)
    bits = int(math.log2(count))
    value = total.reshape((2,) * bits + (total.shape[0] // count, total.shape[1]))
    left = list(range(bits))
    for bunch in rounds:
        dims = [left.index(b) for b in bunch]
        value = jnp.moveaxis(value, dims, range(len(bunch)))
        rest = value.shape[len(bunch):]
        value = value.reshape((2 ** len(bunch),) + rest)
        mine = jnp.int32(0)
        for b in bunch:
            mine = mine * 2 + ((me >> (bits - 1 - b)) & 1)
        acc = lax.dynamic_index_in_dim(value, mine, 0, keepdims=False)
        for mask in range(1, 2 ** len(bunch)):
            flip = 0
            for place, b in enumerate(bunch):
                if (mask >> (len(bunch) - 1 - place)) & 1:
                    flip |= 1 << (bits - 1 - b)
            acc = acc + crossed(lax.dynamic_index_in_dim(value, mine ^ mask, 0, keepdims=False), axes, flip)
        value = acc
        for b in bunch:
            left.remove(b)
    return value


def local(state_tiles, sketch, probe_cell, probe_row):
    n_tiles = lax.axis_size("sensor")
    width = state_tiles.shape[1]
    steps_here = width // INPUTS
    probe_row = probe_row[0]
    *parts, first, second, swap = pick_rows(state_tiles, probe_cell[0], probe_row)
    arrived = [parts[0]] + [crossed(parts[m], ("sensor",), m) for m in range(1, n_tiles)]
    swapped = crossed(swap, ("tm",), 1)
    back = shifted(first, "tm", 2)
    ahead = shifted(second, "tm", -2)
    own_block = place_rows(probe_row, arrived)
    blocks = [own_block, shifted(own_block, "tm", -1), shifted(own_block, "tm", -2)]
    scale = 1.0 / math.sqrt(SENS_DEV * n_tiles * steps_here * lax.axis_size("tm"))
    place = lax.axis_index("tm").astype(jnp.int32).reshape(1)
    total = gram_image(place, first, second, back, ahead, swapped, arrived, sketch, scale)
    hankel_sketch = hankel_times(blocks, widen(sketch))
    tm_bits = int(math.log2(lax.axis_size("tm")))
    sensor_bits = int(math.log2(n_tiles))
    last = tm_bits + sensor_bits - 1
    rounds = [[last], list(range(tm_bits - 1, last)), list(range(tm_bits - 1))]
    column_image = reduce_scatter(total, ("tm", "sensor"), rounds)
    return (hankel_sketch, column_image)


def solution(mesh):
    placed = (P("sensor", "tm"), P(), P("sensor", None, None), P("sensor", None, None))
    return jax.shard_map(
        local,
        mesh=mesh,
        in_specs=placed,
        out_specs=(P("tm", "sensor", None), P(("tm", "sensor"), None)),
        check_vma=False,
    )
```

```python
import math

import jax
import jax.numpy as jnp
from jax import lax
from jax.experimental import pallas as pl
from jax.experimental.pallas import tpu as pltpu
from jax.sharding import PartitionSpec as P

INPUTS = 16
SENS_DEV = 256
LANES = 128
TAIL = 16
MIB = 1024 * 1024
F32 = jnp.float32
BF16 = jnp.bfloat16


def costs(flops, bytes_accessed=0):
    return pl.CostEstimate(flops=int(flops), bytes_accessed=int(bytes_accessed), transcendentals=0)


def shifted(x, axis, by):
    count = lax.axis_size(axis)
    pairs = [(i, i + by) for i in range(count) if 0 <= i + by < count]
    return lax.ppermute(x, axis, pairs)


def paired(x, axis, by, odd):
    count = lax.axis_size(axis)
    low = [i for i in range(count - by) if (i // by) % 2 == odd]
    return lax.ppermute(x, axis, [(i, i + by) for i in low] + [(i + by, i) for i in low])


def crossed(x, axes, mask):
    count = math.prod(lax.axis_size(a) for a in axes)
    return lax.ppermute(x, axes, [(i, i ^ mask) for i in range(count)])


def pick_rows(state_tiles, probe_cell, probe_row):
    cells_here, width = state_tiles.shape
    tiles, capacity = probe_cell.shape
    rows = tiles * capacity
    steps = 4
    chunk = cells_here // steps

    def kernel(cell_ref, row_ref, state_ref, *refs):
        parts = refs[:tiles]
        slot, total = refs[tiles:]
        k = pl.program_id(0)
        me = lax.axis_index("sensor")

        @pl.when(k == 0)
        def _():
            for m in range(tiles):
                line = cell_ref[pl.ds(me ^ m, 1), :]
                slot[m * capacity : (m + 1) * capacity, :] = jnp.broadcast_to(line, (LANES, capacity)).T
            total[...] = jnp.zeros_like(total)

        lane = lax.broadcasted_iota(jnp.int32, (rows, LANES), 1) + k * chunk
        wanted = slot[...]
        chosen = jnp.concatenate(
            [jnp.where(wanted == lane + c, 1.0, 0.0).astype(BF16) for c in range(0, chunk, LANES)], axis=1
        )
        total[...] += jnp.dot(chosen, state_ref[...], preferred_element_type=F32)

        @pl.when(k == steps - 1)
        def _():
            got = total[...].astype(BF16)
            for m in range(tiles):
                parts[m][:capacity, :] = got[m * capacity : (m + 1) * capacity]
                filled = jnp.broadcast_to(row_ref[pl.ds(me ^ m, 1), :1], (TAIL, width)) >= 0
                parts[m][capacity:, :] = jnp.where(filled, 1.0, 0.0).astype(BF16)

    whole = lambda shape: pl.BlockSpec(shape, lambda k: (0,) * len(shape))
    shapes = [(capacity + TAIL, width)] * tiles
    return pl.pallas_call(
        kernel,
        grid=(steps,),
        in_specs=[whole(probe_cell.shape), whole(probe_row.shape), pl.BlockSpec((chunk, width), lambda k: (k, 0))],
        out_specs=[whole(s) for s in shapes],
        out_shape=[jax.ShapeDtypeStruct(s, BF16) for s in shapes],
        scratch_shapes=[pltpu.VMEM((rows, LANES), jnp.int32), pltpu.VMEM((rows, width), F32)],
        compiler_params=pltpu.CompilerParams(vmem_limit_bytes=10 * MIB),
        cost_estimate=costs(2 * rows * cells_here * width, 2 * cells_here * width),
    )(probe_cell, probe_row, state_tiles)


def place_rows(probe_row, parts):
    tiles, capacity = probe_row.shape
    width = parts[0].shape[1]

    def kernel(row_ref, *refs):
        out_ref = refs[tiles]
        me = lax.axis_index("sensor")
        sensor = lax.broadcasted_iota(jnp.int32, (SENS_DEV, capacity), 0)
        total = jnp.zeros((SENS_DEV, width), F32)
        for m in range(tiles):
            chosen = jnp.where(row_ref[pl.ds(me ^ m, 1), :] == sensor, 1.0, 0.0).astype(BF16)
            total += jnp.dot(chosen, refs[m][:capacity, :], preferred_element_type=F32)
        out_ref[...] = total.astype(BF16)

    return pl.pallas_call(
        kernel,
        out_shape=jax.ShapeDtypeStruct((SENS_DEV, width), BF16),
        compiler_params=pltpu.CompilerParams(vmem_limit_bytes=8 * MIB),
        cost_estimate=costs(2e10),
    )(probe_row, *parts)


def prepare(parts):
    tiles = len(parts)
    capacity, width = parts[0].shape
    capacity -= TAIL
    half = tiles * capacity // 2

    def kernel(*refs):
        first, second, swap, even_pair, odd_pair = refs[tiles:]
        spot = lax.axis_index("tm")
        odd = lax.rem(spot, 2)
        upper = lax.rem(spot // 2, 2)
        for m in range(tiles):
            base = 0 if m < tiles // 2 else half
            at = slice(m * capacity - base, (m + 1) * capacity - base)
            side = first if m < tiles // 2 else second
            side[at, :] = refs[m][:capacity, :]

        @pl.when(odd == 0)
        def _():
            swap[...] = first[...]

        @pl.when(odd == 1)
        def _():
            swap[...] = second[...]

        @pl.when(upper == 0)
        def _():
            even_pair[...] = first[...]
            odd_pair[...] = second[...]

        @pl.when(upper == 1)
        def _():
            even_pair[...] = second[...]
            odd_pair[...] = first[...]

    shapes = [(half, width)] * 5
    return pl.pallas_call(
        kernel,
        out_shape=[jax.ShapeDtypeStruct(s, BF16) for s in shapes],
        compiler_params=pltpu.CompilerParams(vmem_limit_bytes=8 * MIB),
        cost_estimate=costs(5e8),
    )(*parts)


def hankel_times(blocks, sketch):
    rows, width = blocks[0].shape
    span, columns = sketch.shape
    group = LANES // INPUTS
    groups = width // LANES
    reach = span + LANES
    n_blocks = len(blocks)

    def kernel(*refs):
        sketch_ref, out_ref, ext, wide = refs[n_blocks:]
        g = pl.program_id(0)

        @pl.when(g == 0)
        def _():
            for b in range(n_blocks):
                ext[:, b * width : (b + 1) * width] = refs[b][...]
            for o in range(group):
                at = slice(o * columns, (o + 1) * columns)
                top = o * INPUTS
                wide[top : top + span, at] = sketch_ref[...]
                if o:
                    wide[:top, at] = jnp.zeros((top, columns), BF16)
                wide[top + span :, at] = jnp.zeros((LANES - top, columns), BF16)

        window = ext[:, pl.ds(pl.multiple_of(g * LANES, LANES), reach)]
        image = jnp.dot(window, wide[...], preferred_element_type=F32)
        for o in range(group):
            out_ref[o] = image[:, o * columns : (o + 1) * columns]

    return pl.pallas_call(
        kernel,
        grid=(groups,),
        in_specs=[pl.BlockSpec((rows, width), lambda g: (0, 0))] * n_blocks
        + [pl.BlockSpec(sketch.shape, lambda g: (0, 0))],
        out_specs=pl.BlockSpec((group, rows, columns), lambda g: (g, 0, 0)),
        out_shape=jax.ShapeDtypeStruct((groups * group, rows, columns), F32),
        scratch_shapes=[
            pltpu.VMEM((rows, n_blocks * width), BF16),
            pltpu.VMEM((reach, group * columns), BF16),
        ],
        compiler_params=pltpu.CompilerParams(vmem_limit_bytes=13 * MIB),
        cost_estimate=costs(2 * groups * rows * reach * group * columns, 4 * groups * rows * group * columns),
    )(*blocks, sketch)


def across(a, b):
    return lax.dot_general(a, b, (((0,), (0,)), ((), ())), preferred_element_type=F32)


def gram_image(place, first, second, even_pair, odd_pair, swap, parts, sketch, scale):
    half, width = first.shape
    span, columns = sketch.shape
    tiles = len(parts)
    capacity = 2 * half // tiles
    group = LANES // INPUTS
    pair = 2 * LANES
    groups = span // LANES

    def kernel(place_ref, first_ref, second_ref, even_ref, odd_ref, swap_ref, *refs):
        part_refs = refs[:tiles]
        sketch_ref, image_ref, own, left, right, lag, early, full, turned = refs[tiles:]
        spot = place_ref[0]
        odd = lax.rem(spot, 2)
        for m in range(tiles):
            at = slice(m * capacity, (m + 1) * capacity)
            source, base = (first_ref, 0) if m < tiles // 2 else (second_ref, half)
            keep = part_refs[m][capacity : capacity + TAIL, :][:1]
            own[at, :] = source[m * capacity - base : (m + 1) * capacity - base, :] * keep

        upper = lax.rem(spot // 2, 2)

        @pl.when(upper == 0)
        def _():
            left[2 * half : 3 * half, :] = odd_ref[...]
            right[3 * half :, :] = even_ref[...]

        @pl.when(upper == 1)
        def _():
            left[2 * half : 3 * half, :] = even_ref[...]
            right[3 * half :, :] = odd_ref[...]

        left[3 * half :, :] = own[half:, :]
        right[2 * half : 3 * half, :] = own[:half, :]

        @pl.when(odd == 0)
        def _():
            for m in range(tiles // 2, tiles):
                at = slice(m * capacity - half, (m + 1) * capacity - half)
                keep = part_refs[m][capacity : capacity + TAIL, :][:1]
                mine = swap_ref[at, :] * keep
                right[at, :] = mine
                left[half + m * capacity - half : half + (m + 1) * capacity - half, :] = mine
            left[:half, :] = own[half:, :]
            right[half : 2 * half, :] = right[3 * half :, :]

        @pl.when(odd == 1)
        def _():
            for m in range(tiles // 2):
                at = slice(m * capacity, (m + 1) * capacity)
                keep = part_refs[m][capacity : capacity + TAIL, :][:1]
                mine = swap_ref[at, :] * keep
                left[at, :] = mine
                right[half + m * capacity : half + (m + 1) * capacity, :] = mine
            right[:half, :] = own[:half, :]
            left[half : 2 * half, :] = left[2 * half : 3 * half, :]

        lag[...] = jnp.zeros_like(lag)

        @pl.when(spot < 2)
        def _():
            early[...] = jnp.zeros_like(early)

        for q in range(width // pair):
            at = slice(q * pair, (q + 1) * pair)
            low = q * pair
            same = across(own[:, at], own[:, low:])
            n = width - low
            lag[:, :n] += same[:LANES]
            lag[:, : n - LANES] += same[LANES:, LANES:]
            near = across(left[:half, at], right[:half, :])
            one = near + across(left[half : 2 * half, at], right[half : 2 * half, :])
            lag[:, n : n + width] += one[:LANES]
            lag[:, n - LANES : n - LANES + width] += one[LANES:]
            two = across(left[2 * half :, at], right[2 * half :, : low + pair])
            lag[:, n + width :] += two[:LANES, : low + LANES]
            lag[:, n + width - LANES :] += two[LANES:, :]

            @pl.when(spot == 0)
            def _():
                early[at, low:width] = same
                early[at, width : 2 * width] = near

            @pl.when(spot == 1)
            def _():
                early[width + low : width + low + pair, width + low : 2 * width] = same
                early[at, width : 2 * width] = near

        strip = lag[:INPUTS, :span]
        for o in range(1, group):
            strip += pltpu.roll(lag[o * INPUTS : (o + 1) * INPUTS, :], span + LANES - o * INPUTS, 1)[:, :span]
        lane = lax.broadcasted_iota(jnp.int32, strip.shape, 1)
        strip = jnp.where(lane < INPUTS, 0.5 * strip, strip)
        for o in range(group):
            moved = strip if o == 0 else jnp.where(lane < o * INPUTS, 0.0, pltpu.roll(strip, o * INPUTS, 1))
            lag[o * INPUTS : (o + 1) * INPUTS, :span] = moved
        for j in range(groups):
            full[j * LANES : (j + 1) * LANES, j * LANES :] = lag[:, : span - j * LANES]
            if j % 2:
                full[j * LANES : (j + 1) * LANES, (j - 1) * LANES : j * LANES] = jnp.zeros((LANES, LANES), F32)

        @pl.when(spot < 2)
        def _():
            r = lax.broadcasted_iota(jnp.int32, (LANES, LANES), 0) // INPUTS
            c = lax.broadcasted_iota(jnp.int32, (LANES, LANES), 1) // INPUTS
            weight = jnp.where(c > r, 1.0, jnp.where(c == r, 0.5, 0.0))
            for j in range(groups):
                at = slice(j * LANES, (j + 1) * LANES)
                early[at, at] = early[at, at] * weight
                full[at, at] += early[at, at]
                if j + 1 < groups:
                    rest = slice((j + 1) * LANES, span)
                    full[at, rest] += early[at, rest]
            by = 1
            while by < group:
                step = by * INPUTS
                for j in reversed(range(groups)):
                    at = slice(j * LANES, (j + 1) * LANES)
                    if j:
                        source = early[j * LANES - step : (j + 1) * LANES - step, (j - 1) * LANES :]
                        early[at, j * LANES :] += pltpu.roll(source, step, 1)[:, LANES:]
                    else:
                        source = early[: LANES - step, :]
                        early[step:LANES, :] += pltpu.roll(source, step, 1)
                by *= 2
            by = 1
            while by < groups:
                for j in reversed(range(by, groups)):
                    early[j * LANES : (j + 1) * LANES, j * LANES :] += early[
                        (j - by) * LANES : (j - by + 1) * LANES, (j - by) * LANES : span - by * LANES
                    ]
                by *= 2
            for j in range(groups):
                at = slice(j * LANES, (j + 1) * LANES)
                full[at, at] -= jnp.where(c >= r, early[at, at], 0.0)
                if j + 1 < groups:
                    rest = slice((j + 1) * LANES, span)
                    full[at, rest] -= early[at, rest]

        for q in range(span // pair):
            at = slice(q * pair, (q + 1) * pair)
            value = full[at, q * pair :]
            high = value.astype(BF16)
            low = (value - high.astype(F32)).astype(BF16)
            below = sketch_ref[q * pair :, :]
            image_ref[at, :] = jnp.dot(high, below, preferred_element_type=F32) + jnp.dot(
                low, below, preferred_element_type=F32
            )
            tall = sketch_ref[at, :]
            down = across(tall, high) + across(tall, low)
            if q == 0:
                turned[...] = down
            else:
                turned[:, q * pair :] += down
        image_ref[...] = (image_ref[...] + turned[...].T) * scale

    vmem = pl.BlockSpec(memory_space=pltpu.VMEM)
    smem = pl.BlockSpec(memory_space=pltpu.SMEM)
    return pl.pallas_call(
        kernel,
        in_specs=[smem] + [vmem] * (6 + tiles),
        out_specs=vmem,
        out_shape=jax.ShapeDtypeStruct((span, columns), F32),
        scratch_shapes=[
            pltpu.VMEM((2 * half, width), BF16),
            pltpu.VMEM((4 * half, width), BF16),
            pltpu.VMEM((4 * half, width), BF16),
            pltpu.VMEM((LANES, span + LANES), F32),
            pltpu.VMEM((span, span), F32),
            pltpu.VMEM((span, span), F32),
            pltpu.VMEM((columns, span), F32),
        ],
        compiler_params=pltpu.CompilerParams(vmem_limit_bytes=18 * MIB),
        cost_estimate=costs(5e9),
    )(place, first, second, even_pair, odd_pair, swap, *parts, sketch)


def reduce_scatter(total, axes, rounds, left=None, gate=None):
    count = math.prod(lax.axis_size(a) for a in axes)
    me = jnp.int32(0)
    for a in axes:
        me = me * lax.axis_size(a) + lax.axis_index(a)
    bits = int(math.log2(count))
    left = list(range(bits)) if left is None else left
    value = total
    if value.ndim == 2:
        value = total.reshape((2,) * bits + (total.shape[0] // count, total.shape[1]))
    for bunch in rounds:
        dims = [left.index(b) for b in bunch]
        value = jnp.moveaxis(value, dims, range(len(bunch)))
        rest = value.shape[len(bunch):]
        value = value.reshape((2 ** len(bunch),) + rest)
        mine = jnp.int32(0)
        for b in bunch:
            mine = mine * 2 + ((me >> (bits - 1 - b)) & 1)
        acc = lax.dynamic_index_in_dim(value, mine, 0, keepdims=False)
        came = []
        for mask in range(1, 2 ** len(bunch)):
            flip = 0
            for place, b in enumerate(bunch):
                if (mask >> (len(bunch) - 1 - place)) & 1:
                    flip |= 1 << (bits - 1 - b)
            piece = lax.dynamic_index_in_dim(value, mine ^ mask, 0, keepdims=False)
            if len(bunch) == 1:
                came.append(jnp.stack([crossed(part, axes, flip) for part in piece]))
            else:
                came.append(crossed(piece, axes, flip))
        if gate is not None and len(left) == len(bunch):
            came, gate = lax.optimization_barrier((came, gate))
        for piece in came:
            acc = acc + piece
        value = acc
        for b in bunch:
            left.remove(b)
    return value if gate is None else (value, gate)


def local(state_tiles, sketch, probe_cell, probe_row):
    n_tiles = lax.axis_size("sensor")
    width = state_tiles.shape[1]
    steps_here = width // INPUTS
    probe_row = probe_row[0]
    parts = pick_rows(state_tiles, probe_cell[0], probe_row)
    arrived = [parts[0]] + [crossed(parts[m], ("sensor",), m) for m in range(1, n_tiles)]
    first, second, swap, even_pair, odd_pair = prepare(parts)
    swapped = crossed(swap, ("tm",), 1)
    even_pair = paired(even_pair, "tm", 2, 0)
    odd_pair = paired(odd_pair, "tm", 2, 1)
    own_block = place_rows(probe_row, arrived)
    own_block, first = lax.optimization_barrier((own_block, first))
    next_two = shifted(own_block, "tm", -2)
    scale = 1.0 / math.sqrt(SENS_DEV * n_tiles * steps_here * lax.axis_size("tm"))
    place = lax.axis_index("tm").astype(jnp.int32).reshape(1)
    total = gram_image(place, first, second, even_pair, odd_pair, swapped, arrived, sketch, scale)
    tm_bits = int(math.log2(lax.axis_size("tm")))
    sensor_bits = int(math.log2(n_tiles))
    last = tm_bits + sensor_bits - 1
    axes = ("tm", "sensor")
    total = reduce_scatter(total, axes, [[last]])
    total, next_two = lax.optimization_barrier((total, next_two))
    next_one = crossed(jnp.where(lax.rem(place[0], 2) == 0, next_two, own_block), ("tm",), 1)
    hankel_sketch = hankel_times([own_block, next_one, next_two], sketch)
    rounds = [list(range(tm_bits - 1, last)), list(range(tm_bits - 1))]
    column_image, hankel_sketch = reduce_scatter(total, axes, rounds, list(range(last)), hankel_sketch)
    return (hankel_sketch, column_image)


def solution(mesh):
    placed = (P("sensor", "tm"), P(), P("sensor", None, None), P("sensor", None, None))
    return jax.shard_map(
        local,
        mesh=mesh,
        in_specs=placed,
        out_specs=(P("tm", "sensor", None), P(("tm", "sensor"), None)),
        check_vma=False,
    )
```

```python
import math

import jax
import jax.numpy as jnp
from jax import lax
from jax.experimental import pallas as pl
from jax.experimental.pallas import tpu as pltpu
from jax.sharding import PartitionSpec as P

INPUTS = 16
SENS_DEV = 256
LANES = 128
TAIL = 16
MIB = 1024 * 1024
F32 = jnp.float32
BF16 = jnp.bfloat16


def costs(flops, bytes_accessed=0):
    return pl.CostEstimate(flops=int(flops), bytes_accessed=int(bytes_accessed), transcendentals=0)


def shifted(x, axis, by):
    count = lax.axis_size(axis)
    pairs = [(i, i + by) for i in range(count) if 0 <= i + by < count]
    return lax.ppermute(x, axis, pairs)


def paired(x, by, odd):
    count, width = lax.axis_size("tm"), lax.axis_size("sensor")
    low = [i for i in range(count - by) if (i // by) % 2 == odd]
    partner = {i: i + by for i in low} | {i + by: i for i in low}
    pairs = []
    for i in range(count):
        for j in range(width):
            target = partner[i] * width + j if i in partner else i * width + (j ^ 1)
            pairs.append((i * width + j, target))
    return lax.ppermute(x, ("tm", "sensor"), pairs)


def crossed(x, axes, mask):
    count = math.prod(lax.axis_size(a) for a in axes)
    return lax.ppermute(x, axes, [(i, i ^ mask) for i in range(count)])


def pick_rows(state_tiles, probe_cell, probe_row):
    cells_here, width = state_tiles.shape
    tiles, capacity = probe_cell.shape
    rows = tiles * capacity
    steps = 4
    chunk = cells_here // steps

    def kernel(cell_hbm, row_hbm, state_hbm, *refs):
        parts = refs[:tiles]
        row_ref, cell_ref, slot, total, state, came = refs[tiles:]
        me = lax.axis_index("sensor")
        copies = [pltpu.make_async_copy(cell_hbm, cell_ref, came.at[steps])]
        copies.append(pltpu.make_async_copy(row_hbm, row_ref, came.at[steps + 1]))
        for k in range(steps):
            at = slice(k * chunk, (k + 1) * chunk)
            copies.append(pltpu.make_async_copy(state_hbm.at[at, :], state.at[at, :], came.at[k]))
        for copy in copies:
            copy.start()
        copies[0].wait()
        copies[1].wait()
        for m in range(tiles):
            line = cell_ref[pl.ds(me ^ m, 1), :]
            slot[m * capacity : (m + 1) * capacity, :] = jnp.broadcast_to(line, (LANES, capacity)).T
        lane = lax.broadcasted_iota(jnp.int32, (rows, LANES), 1)
        for k in range(steps):
            wanted = slot[...]
            chosen = jnp.concatenate(
                [jnp.where(wanted == lane + c, 1.0, 0.0).astype(BF16) for c in range(k * chunk, (k + 1) * chunk, LANES)],
                axis=1,
            )
            copies[2 + k].wait()
            got = jnp.dot(chosen, state[k * chunk : (k + 1) * chunk, :], preferred_element_type=F32)
            if k:
                got += total[...]
            if k < steps - 1:
                total[...] = got
        got = got.astype(BF16)
        for m in range(tiles):
            parts[m][:capacity, :] = got[m * capacity : (m + 1) * capacity]
            filled = jnp.broadcast_to(row_ref[pl.ds(me ^ m, 1), :1], (TAIL, width)) >= 0
            parts[m][capacity:, :] = jnp.where(filled, 1.0, 0.0).astype(BF16)

    shapes = [(capacity + TAIL, width)] * tiles
    return pl.pallas_call(
        kernel,
        in_specs=[pl.BlockSpec(memory_space=pltpu.HBM)] * 3,
        out_specs=[pl.BlockSpec(memory_space=pltpu.VMEM)] * (tiles + 1),
        out_shape=[jax.ShapeDtypeStruct(s, BF16) for s in shapes] + [jax.ShapeDtypeStruct(probe_row.shape, jnp.int32)],
        scratch_shapes=[
            pltpu.VMEM(probe_cell.shape, jnp.int32),
            pltpu.VMEM((rows, LANES), jnp.int32),
            pltpu.VMEM((rows, width), F32),
            pltpu.VMEM((cells_here, width), BF16),
            pltpu.SemaphoreType.DMA((steps + 2,)),
        ],
        compiler_params=pltpu.CompilerParams(vmem_limit_bytes=10 * MIB),
        cost_estimate=costs(2 * rows * cells_here * width, 2 * cells_here * width),
    )(*[pltpu.with_memory_space_constraint(x, pltpu.HBM) for x in (probe_cell, probe_row, state_tiles)])


def place_rows(wanted, parts):
    tiles, capacity = wanted.shape
    width = parts[0].shape[1]

    def kernel(row_ref, *refs):
        out_ref = refs[tiles]
        me = lax.axis_index("sensor")
        sensor = lax.broadcasted_iota(jnp.int32, (SENS_DEV, capacity), 0)
        total = jnp.zeros((SENS_DEV, width), F32)
        for m in range(tiles):
            chosen = jnp.where(row_ref[pl.ds(me ^ m, 1), :] == sensor, 1.0, 0.0).astype(BF16)
            total += jnp.dot(chosen, refs[m][:capacity, :], preferred_element_type=F32)
        out_ref[...] = total.astype(BF16)

    return pl.pallas_call(
        kernel,
        out_shape=jax.ShapeDtypeStruct((SENS_DEV, width), BF16),
        compiler_params=pltpu.CompilerParams(vmem_limit_bytes=8 * MIB),
        cost_estimate=costs(2e10),
    )(wanted, *parts)


def prepare(parts):
    tiles = len(parts)
    capacity, width = parts[0].shape
    capacity -= TAIL
    half = tiles * capacity // 2

    def kernel(*refs):
        first, second, swap, even_pair, odd_pair = refs[tiles:]
        spot = lax.axis_index("tm")
        odd = lax.rem(spot, 2)
        upper = lax.rem(spot // 2, 2)
        for m in range(tiles):
            base = 0 if m < tiles // 2 else half
            at = slice(m * capacity - base, (m + 1) * capacity - base)
            side = first if m < tiles // 2 else second
            side[at, :] = refs[m][:capacity, :]

        @pl.when(odd == 0)
        def _():
            swap[...] = first[...]

        @pl.when(odd == 1)
        def _():
            swap[...] = second[...]

        @pl.when(upper == 0)
        def _():
            even_pair[...] = first[...]
            odd_pair[...] = second[...]

        @pl.when(upper == 1)
        def _():
            even_pair[...] = second[...]
            odd_pair[...] = first[...]

    shapes = [(half, width)] * 5
    return pl.pallas_call(
        kernel,
        out_shape=[jax.ShapeDtypeStruct(s, BF16) for s in shapes],
        compiler_params=pltpu.CompilerParams(vmem_limit_bytes=8 * MIB),
        cost_estimate=costs(5e8),
    )(*parts)


def hankel_ends(first, last, sketch):
    rows, width = first.shape
    span, columns = sketch.shape
    group = LANES // INPUTS
    groups = width // LANES

    def kernel(first_ref, last_ref, sketch_ref, out_ref, wide):
        for o in range(group):
            at = slice(o * columns, (o + 1) * columns)
            top = o * INPUTS
            wide[top : top + span, at] = sketch_ref[...]
            if o:
                wide[:top, at] = jnp.zeros((top, columns), BF16)
            wide[top + span :, at] = jnp.zeros((LANES - top, columns), BF16)
        for g in range(groups):
            shift = g * LANES
            image = jnp.dot(first_ref[:, shift:], wide[: width - shift, :], preferred_element_type=F32)
            image += jnp.dot(last_ref[:, : shift + LANES], wide[span - shift :, :], preferred_element_type=F32)
            for o in range(group):
                out_ref[g * group + o] = image[:, o * columns : (o + 1) * columns]

    vmem = pl.BlockSpec(memory_space=pltpu.VMEM)
    return pl.pallas_call(
        kernel,
        in_specs=[vmem] * 3,
        out_specs=[vmem] * 2,
        out_shape=[
            jax.ShapeDtypeStruct((groups * group, rows, columns), F32),
            jax.ShapeDtypeStruct((span + LANES, group * columns), BF16),
        ],
        compiler_params=pltpu.CompilerParams(vmem_limit_bytes=8 * MIB),
        cost_estimate=costs(2.5e9),
    )(first, last, sketch)


def hankel_middle(middle, wide, ends):
    rows, width = middle.shape
    group = LANES // INPUTS
    groups = width // LANES
    columns = ends.shape[2]

    def kernel(middle_ref, wide_ref, ends_ref, out_hbm, result, sent):
        copies = []
        for g in range(groups):
            at = slice(width - g * LANES, 2 * width - g * LANES)
            image = jnp.dot(middle_ref[...], wide_ref[at, :], preferred_element_type=F32)
            for o in range(group):
                i = g * group + o
                result[i] = image[:, o * columns : (o + 1) * columns] + ends_ref[i]
                copies.append(pltpu.make_async_copy(result.at[i], out_hbm.at[i], sent.at[i]))
                copies[-1].start()
        for copy in copies:
            copy.wait()

    vmem = pl.BlockSpec(memory_space=pltpu.VMEM)
    return pl.pallas_call(
        kernel,
        in_specs=[vmem] * 3,
        out_specs=pl.BlockSpec(memory_space=pltpu.HBM),
        out_shape=jax.ShapeDtypeStruct(ends.shape, F32),
        scratch_shapes=[pltpu.VMEM(ends.shape, F32), pltpu.SemaphoreType.DMA((groups * group,))],
        compiler_params=pltpu.CompilerParams(vmem_limit_bytes=8 * MIB),
        cost_estimate=costs(2.5e9),
    )(middle, wide, ends)


def across(a, b):
    return lax.dot_general(a, b, (((0,), (0,)), ((), ())), preferred_element_type=F32)


def gram_image(place, first, second, even_pair, odd_pair, swap, parts, sketch, scale):
    half, width = first.shape
    span, columns = sketch.shape
    tiles = len(parts)
    capacity = 2 * half // tiles
    places = lax.axis_size("tm")
    group = LANES // INPUTS
    pair = 2 * LANES
    groups = span // LANES

    def kernel(place_ref, first_ref, second_ref, even_ref, odd_ref, swap_ref, *refs):
        part_refs = refs[:tiles]
        sketch_ref, image_ref, own, left, right, lag, early, full, turned = refs[tiles:]
        spot = place_ref[0]
        odd = lax.rem(spot, 2)
        for m in range(tiles):
            at = slice(m * capacity, (m + 1) * capacity)
            source, base = (first_ref, 0) if m < tiles // 2 else (second_ref, half)
            keep = part_refs[m][capacity : capacity + TAIL, :][:1]
            own[at, :] = source[m * capacity - base : (m + 1) * capacity - base, :] * keep

        upper = lax.rem(spot // 2, 2)

        @pl.when(upper == 0)
        def _():
            left[2 * half : 3 * half, :] = odd_ref[...]
            right[3 * half :, :] = even_ref[...]

        @pl.when(upper == 1)
        def _():
            left[2 * half : 3 * half, :] = even_ref[...]
            right[3 * half :, :] = odd_ref[...]

        @pl.when(spot < 2)
        def _():
            left[2 * half : 3 * half, :] = jnp.zeros((half, width), BF16)

        @pl.when(spot >= places - 2)
        def _():
            right[3 * half :, :] = jnp.zeros((half, width), BF16)

        left[3 * half :, :] = own[half:, :]
        right[2 * half : 3 * half, :] = own[:half, :]

        @pl.when(odd == 0)
        def _():
            for m in range(tiles // 2, tiles):
                at = slice(m * capacity - half, (m + 1) * capacity - half)
                keep = part_refs[m][capacity : capacity + TAIL, :][:1]
                mine = swap_ref[at, :] * keep
                right[at, :] = mine
                left[half + m * capacity - half : half + (m + 1) * capacity - half, :] = mine
            left[:half, :] = own[half:, :]
            right[half : 2 * half, :] = right[3 * half :, :]

        @pl.when(odd == 1)
        def _():
            for m in range(tiles // 2):
                at = slice(m * capacity, (m + 1) * capacity)
                keep = part_refs[m][capacity : capacity + TAIL, :][:1]
                mine = swap_ref[at, :] * keep
                left[at, :] = mine
                right[half + m * capacity : half + (m + 1) * capacity, :] = mine
            right[:half, :] = own[:half, :]
            left[half : 2 * half, :] = left[2 * half : 3 * half, :]

        lag[...] = jnp.zeros_like(lag)

        for q in range(width // pair):
            at = slice(q * pair, (q + 1) * pair)
            low = q * pair
            same = across(own[:, at], own[:, low:])
            n = width - low
            lag[:, :n] += same[:LANES]
            lag[:, : n - LANES] += same[LANES:, LANES:]
            near = across(left[:half, at], right[:half, :])
            one = near + across(left[half : 2 * half, at], right[half : 2 * half, :])
            lag[:, n : n + width] += one[:LANES]
            lag[:, n - LANES : n - LANES + width] += one[LANES:]
            two = across(left[2 * half :, at], right[2 * half :, : low + pair])
            lag[:, n + width :] += two[:LANES, : low + LANES]
            lag[:, n + width - LANES :] += two[LANES:, :]

            @pl.when(spot == 0)
            def _():
                early[at, low:width] = same
                early[at, width : 2 * width] = near

            @pl.when(spot == 1)
            def _():
                early[width + low : width + low + pair, width + low : 2 * width] = same
                early[at, width : 2 * width] = near

        strip = lag[:INPUTS, :span]
        for o in range(1, group):
            strip += pltpu.roll(lag[o * INPUTS : (o + 1) * INPUTS, :], span + LANES - o * INPUTS, 1)[:, :span]
        lane = lax.broadcasted_iota(jnp.int32, strip.shape, 1)
        strip = jnp.where(lane < INPUTS, 0.5 * strip, strip)
        for o in range(group):
            moved = strip if o == 0 else jnp.where(lane < o * INPUTS, 0.0, pltpu.roll(strip, o * INPUTS, 1))
            lag[o * INPUTS : (o + 1) * INPUTS, :span] = moved
        for j in range(1, groups, 2):
            full[j * LANES : (j + 1) * LANES, (j - 1) * LANES : j * LANES] = jnp.zeros((LANES, LANES), F32)

        @pl.when(spot >= 2)
        def _():
            for j in range(groups):
                full[j * LANES : (j + 1) * LANES, j * LANES :] = lag[:, : span - j * LANES]

        @pl.when(spot < 2)
        def _():
            r = lax.broadcasted_iota(jnp.int32, (LANES, LANES), 0) // INPUTS
            c = lax.broadcasted_iota(jnp.int32, (LANES, LANES), 1) // INPUTS
            weight = jnp.where(c > r, 1.0, jnp.where(c == r, 0.5, 0.0))
            blocks_here = width // LANES

            @pl.when(spot == 0)
            def _():
                for j in range(blocks_here, 2 * blocks_here):
                    at = slice(j * LANES, (j + 1) * LANES)
                    early[at, j * LANES :] = jnp.zeros((LANES, span - j * LANES), F32)

            @pl.when(spot == 1)
            def _():
                for j in range(blocks_here):
                    at = slice(j * LANES, (j + 1) * LANES)
                    early[at, j * LANES : width] = jnp.zeros((LANES, width - j * LANES), F32)

            for j in range(groups):
                at = slice(j * LANES, (j + 1) * LANES)
                early[at, at] = early[at, at] * weight
                full[at, j * LANES :] = lag[:, : span - j * LANES] + early[at, j * LANES :]
            for j in range(1, groups):
                early[j * LANES : (j + 1) * LANES, j * LANES :] += early[
                    (j - 1) * LANES : j * LANES, (j - 1) * LANES : span - LANES
                ]
            by = 1
            while by < group:
                step = by * INPUTS
                by *= 2
                for j in reversed(range(groups)):
                    at = slice(j * LANES, (j + 1) * LANES)
                    if j:
                        source = early[j * LANES - step : (j + 1) * LANES - step, (j - 1) * LANES :]
                        value = early[at, j * LANES :] + pltpu.roll(source, step, 1)[:, LANES:]
                    else:
                        source = jnp.concatenate([jnp.zeros((step, span), F32), early[: LANES - step, :]], axis=0)
                        value = early[at, :] + pltpu.roll(source, step, 1)
                    if by < group:
                        early[at, j * LANES :] = value
                    else:
                        full[at, at] -= jnp.where(c >= r, value[:, :LANES], 0.0)
                        if j + 1 < groups:
                            full[at, (j + 1) * LANES :] -= value[:, LANES:]

        for q in range(span // pair):
            at = slice(q * pair, (q + 1) * pair)
            value = full[at, q * pair :]
            high = value.astype(BF16)
            low = (value - high.astype(F32)).astype(BF16)
            below = sketch_ref[q * pair :, :]
            image_ref[at, :] = jnp.dot(high, below, preferred_element_type=F32) + jnp.dot(
                low, below, preferred_element_type=F32
            )
            tall = sketch_ref[at, :]
            down = across(tall, high) + across(tall, low)
            if q == 0:
                turned[...] = down
            else:
                turned[:, q * pair :] += down
        image_ref[...] = (image_ref[...] + turned[...].T) * scale

    vmem = pl.BlockSpec(memory_space=pltpu.VMEM)
    smem = pl.BlockSpec(memory_space=pltpu.SMEM)
    return pl.pallas_call(
        kernel,
        in_specs=[smem] + [vmem] * (6 + tiles),
        out_specs=vmem,
        out_shape=jax.ShapeDtypeStruct((span, columns), F32),
        scratch_shapes=[
            pltpu.VMEM((2 * half, width), BF16),
            pltpu.VMEM((4 * half, width), BF16),
            pltpu.VMEM((4 * half, width), BF16),
            pltpu.VMEM((LANES, span + LANES), F32),
            pltpu.VMEM((span, span), F32),
            pltpu.VMEM((span, span), F32),
            pltpu.VMEM((columns, span), F32),
        ],
        compiler_params=pltpu.CompilerParams(vmem_limit_bytes=18 * MIB),
        cost_estimate=costs(5e9),
    )(place, first, second, even_pair, odd_pair, swap, *parts, sketch)


def reduce_scatter(total, axes, rounds, left=None, gate=None):
    count = math.prod(lax.axis_size(a) for a in axes)
    me = jnp.int32(0)
    for a in axes:
        me = me * lax.axis_size(a) + lax.axis_index(a)
    bits = int(math.log2(count))
    left = list(range(bits)) if left is None else left
    value = total
    if value.ndim == 2:
        value = total.reshape((2,) * bits + (total.shape[0] // count, total.shape[1]))
    for bunch in rounds:
        dims = [left.index(b) for b in bunch]
        value = jnp.moveaxis(value, dims, range(len(bunch)))
        rest = value.shape[len(bunch):]
        value = value.reshape((2 ** len(bunch),) + rest)
        mine = jnp.int32(0)
        for b in bunch:
            mine = mine * 2 + ((me >> (bits - 1 - b)) & 1)
        acc = lax.dynamic_index_in_dim(value, mine, 0, keepdims=False)
        came = []
        for mask in range(1, 2 ** len(bunch)):
            flip = 0
            for place, b in enumerate(bunch):
                if (mask >> (len(bunch) - 1 - place)) & 1:
                    flip |= 1 << (bits - 1 - b)
            piece = lax.dynamic_index_in_dim(value, mine ^ mask, 0, keepdims=False)
            if len(bunch) == 1:
                came.append(jnp.stack([crossed(part, axes, flip) for part in piece]))
            else:
                came.append(crossed(piece, axes, flip))
        if gate is not None and bunch is rounds[-1]:
            came, gate = lax.optimization_barrier((came, gate))
        for piece in came:
            acc = acc + piece
        value = acc
        for b in bunch:
            left.remove(b)
    return value if gate is None else (value, gate)


def local(state_tiles, sketch, probe_cell, probe_row):
    n_tiles = lax.axis_size("sensor")
    width = state_tiles.shape[1]
    steps_here = width // INPUTS
    *parts, wanted = pick_rows(state_tiles, probe_cell[0], probe_row[0])
    arrived = [parts[0]] + [crossed(parts[m], ("sensor",), m) for m in range(1, n_tiles)]
    first, second, swap, even_pair, odd_pair = prepare(parts)
    swapped = crossed(swap, ("tm",), 1)
    odd_pair = paired(odd_pair, 2, 1)
    even_pair = paired(even_pair, 2, 0)
    own_block = place_rows(wanted, arrived)
    own_block, first = lax.optimization_barrier((own_block, first))
    next_two = shifted(own_block, "tm", -2)
    scale = 1.0 / math.sqrt(SENS_DEV * n_tiles * steps_here * lax.axis_size("tm"))
    place = lax.axis_index("tm").astype(jnp.int32).reshape(1)
    total = gram_image(place, first, second, even_pair, odd_pair, swapped, arrived, sketch, scale)
    tm_bits = int(math.log2(lax.axis_size("tm")))
    sensor_bits = int(math.log2(n_tiles))
    last = tm_bits + sensor_bits - 1
    axes = ("tm", "sensor")
    total = reduce_scatter(total, axes, [[last]])
    total, next_two = lax.optimization_barrier((total, next_two))
    next_one = crossed(jnp.where(lax.rem(place[0], 2) == 0, next_two, own_block), ("tm",), 1)
    ends, wide = hankel_ends(own_block, next_two, sketch)
    left = list(range(last))
    total, ends = reduce_scatter(total, axes, [list(range(tm_bits - 1, last))], left, ends)
    hankel_sketch = hankel_middle(next_one, wide, ends)
    left = list(range(tm_bits - 1))
    column_image, hankel_sketch = reduce_scatter(total, axes, [left], list(left), hankel_sketch)
    return (hankel_sketch, column_image)


def solution(mesh):
    placed = (P("sensor", "tm"), P(), P("sensor", None, None), P("sensor", None, None))
    return jax.shard_map(
        local,
        mesh=mesh,
        in_specs=placed,
        out_specs=(P("tm", "sensor", None), P(("tm", "sensor"), None)),
        check_vma=False,
    )
```

```python
import math

import jax
import jax.numpy as jnp
from jax import lax
from jax.experimental import pallas as pl
from jax.experimental.pallas import tpu as pltpu
from jax.sharding import PartitionSpec as P

INPUTS = 16
SENS_DEV = 256
LANES = 128
TAIL = 16
MIB = 1024 * 1024
F32 = jnp.float32
BF16 = jnp.bfloat16


def costs(flops, bytes_accessed=0):
    return pl.CostEstimate(flops=int(flops), bytes_accessed=int(bytes_accessed), transcendentals=0)


def shifted(x, axis, by):
    count = lax.axis_size(axis)
    pairs = [(i, i + by) for i in range(count) if 0 <= i + by < count]
    return lax.ppermute(x, axis, pairs)


def paired(x, by, odd):
    count, width = lax.axis_size("tm"), lax.axis_size("sensor")
    low = [i for i in range(count - by) if (i // by) % 2 == odd]
    partner = {i: i + by for i in low} | {i + by: i for i in low}
    pairs = []
    for i in range(count):
        for j in range(width):
            target = partner[i] * width + j if i in partner else i * width + (j ^ 1)
            pairs.append((i * width + j, target))
    return lax.ppermute(x, ("tm", "sensor"), pairs)


def crossed(x, axes, mask):
    count = math.prod(lax.axis_size(a) for a in axes)
    return lax.ppermute(x, axes, [(i, i ^ mask) for i in range(count)])


def pick_rows(state_tiles, probe_cell, probe_row):
    cells_here, width = state_tiles.shape
    tiles, capacity = probe_cell.shape
    rows = tiles * capacity
    steps = 4
    chunk = cells_here // steps

    def kernel(cell_hbm, row_hbm, state_hbm, *refs):
        parts = refs[:tiles]
        row_ref, cell_ref, slot, total, state, came = refs[tiles:]
        me = lax.axis_index("sensor")
        copies = [pltpu.make_async_copy(cell_hbm, cell_ref, came.at[steps])]
        copies.append(pltpu.make_async_copy(row_hbm, row_ref, came.at[steps + 1]))
        for k in range(steps):
            at = slice(k * chunk, (k + 1) * chunk)
            copies.append(pltpu.make_async_copy(state_hbm.at[at, :], state.at[at, :], came.at[k]))
        for copy in copies:
            copy.start()
        copies[0].wait()
        copies[1].wait()
        for m in range(tiles):
            line = cell_ref[pl.ds(me ^ m, 1), :]
            slot[m * capacity : (m + 1) * capacity, :] = jnp.broadcast_to(line, (LANES, capacity)).T
        lane = lax.broadcasted_iota(jnp.int32, (rows, LANES), 1)
        wanted = slot[...]
        tile = (wanted // LANES).astype(F32).astype(BF16)
        within = jnp.where(lax.rem(wanted, LANES) == lane, 1.0, 0.0).astype(BF16)
        none = jnp.zeros_like(within)
        for k in range(steps):
            chosen = jnp.concatenate(
                [jnp.where(tile == jnp.asarray(c, BF16), within, none) for c in range(k * chunk // LANES, (k + 1) * chunk // LANES)],
                axis=1,
            )
            copies[2 + k].wait()
            got = jnp.dot(chosen, state[k * chunk : (k + 1) * chunk, :], preferred_element_type=F32)
            if k:
                got += total[...]
            if k < steps - 1:
                total[...] = got
        got = got.astype(BF16)
        for m in range(tiles):
            parts[m][:capacity, :] = got[m * capacity : (m + 1) * capacity]
            filled = jnp.broadcast_to(row_ref[pl.ds(me ^ m, 1), :1], (TAIL, width)) >= 0
            parts[m][capacity:, :] = jnp.where(filled, 1.0, 0.0).astype(BF16)

    shapes = [(capacity + TAIL, width)] * tiles
    return pl.pallas_call(
        kernel,
        in_specs=[pl.BlockSpec(memory_space=pltpu.HBM)] * 3,
        out_specs=[pl.BlockSpec(memory_space=pltpu.VMEM)] * (tiles + 1),
        out_shape=[jax.ShapeDtypeStruct(s, BF16) for s in shapes] + [jax.ShapeDtypeStruct(probe_row.shape, jnp.int32)],
        scratch_shapes=[
            pltpu.VMEM(probe_cell.shape, jnp.int32),
            pltpu.VMEM((rows, LANES), jnp.int32),
            pltpu.VMEM((rows, width), F32),
            pltpu.VMEM((cells_here, width), BF16),
            pltpu.SemaphoreType.DMA((steps + 2,)),
        ],
        compiler_params=pltpu.CompilerParams(vmem_limit_bytes=10 * MIB),
        cost_estimate=costs(2 * rows * cells_here * width, 2 * cells_here * width),
    )(*[pltpu.with_memory_space_constraint(x, pltpu.HBM) for x in (probe_cell, probe_row, state_tiles)])


def place_rows(wanted, parts):
    tiles, capacity = wanted.shape
    width = parts[0].shape[1]

    def kernel(row_ref, *refs):
        out_ref = refs[tiles]
        me = lax.axis_index("sensor")
        sensor = lax.broadcasted_iota(jnp.int32, (SENS_DEV, capacity), 0)
        total = jnp.zeros((SENS_DEV, width), F32)
        for m in range(tiles):
            chosen = jnp.where(row_ref[pl.ds(me ^ m, 1), :] == sensor, 1.0, 0.0).astype(BF16)
            total += jnp.dot(chosen, refs[m][:capacity, :], preferred_element_type=F32)
        out_ref[...] = total.astype(BF16)

    return pl.pallas_call(
        kernel,
        out_shape=jax.ShapeDtypeStruct((SENS_DEV, width), BF16),
        compiler_params=pltpu.CompilerParams(vmem_limit_bytes=8 * MIB),
        cost_estimate=costs(2e10),
    )(wanted, *parts)


def prepare(parts):
    tiles = len(parts)
    capacity, width = parts[0].shape
    capacity -= TAIL
    half = tiles * capacity // 2

    def kernel(*refs):
        first, second, swap, even_pair, odd_pair = refs[tiles:]
        spot = lax.axis_index("tm")
        odd = lax.rem(spot, 2)
        upper = lax.rem(spot // 2, 2)
        for m in range(tiles):
            base = 0 if m < tiles // 2 else half
            at = slice(m * capacity - base, (m + 1) * capacity - base)
            side = first if m < tiles // 2 else second
            side[at, :] = refs[m][:capacity, :]

        @pl.when(odd == 0)
        def _():
            swap[...] = first[...]

        @pl.when(odd == 1)
        def _():
            swap[...] = second[...]

        @pl.when(upper == 0)
        def _():
            even_pair[...] = first[...]
            odd_pair[...] = second[...]

        @pl.when(upper == 1)
        def _():
            even_pair[...] = second[...]
            odd_pair[...] = first[...]

    shapes = [(half, width)] * 5
    return pl.pallas_call(
        kernel,
        out_shape=[jax.ShapeDtypeStruct(s, BF16) for s in shapes],
        compiler_params=pltpu.CompilerParams(vmem_limit_bytes=8 * MIB),
        cost_estimate=costs(5e8),
    )(*parts)


def hankel_ends(first, last, sketch):
    rows, width = first.shape
    span, columns = sketch.shape
    group = LANES // INPUTS
    groups = width // LANES

    def kernel(first_ref, last_ref, sketch_ref, out_ref, wide):
        for o in range(group):
            at = slice(o * columns, (o + 1) * columns)
            top = o * INPUTS
            wide[top : top + span, at] = sketch_ref[...]
            if o:
                wide[:top, at] = jnp.zeros((top, columns), BF16)
            wide[top + span :, at] = jnp.zeros((LANES - top, columns), BF16)
        for g in range(groups):
            shift = g * LANES
            image = jnp.dot(first_ref[:, shift:], wide[: width - shift, :], preferred_element_type=F32)
            image += jnp.dot(last_ref[:, : shift + LANES], wide[span - shift :, :], preferred_element_type=F32)
            for o in range(group):
                out_ref[g * group + o] = image[:, o * columns : (o + 1) * columns]

    vmem = pl.BlockSpec(memory_space=pltpu.VMEM)
    return pl.pallas_call(
        kernel,
        in_specs=[vmem] * 3,
        out_specs=[vmem] * 2,
        out_shape=[
            jax.ShapeDtypeStruct((groups * group, rows, columns), F32),
            jax.ShapeDtypeStruct((span + LANES, group * columns), BF16),
        ],
        compiler_params=pltpu.CompilerParams(vmem_limit_bytes=8 * MIB),
        cost_estimate=costs(2.5e9),
    )(first, last, sketch)


def hankel_middle(middle, wide, ends):
    rows, width = middle.shape
    group = LANES // INPUTS
    groups = width // LANES
    columns = ends.shape[2]

    def kernel(middle_ref, wide_ref, ends_ref, out_hbm, result, sent):
        copies = []
        for g in range(groups):
            at = slice(width - g * LANES, 2 * width - g * LANES)
            image = jnp.dot(middle_ref[...], wide_ref[at, :], preferred_element_type=F32)
            for o in range(group):
                i = g * group + o
                result[i] = image[:, o * columns : (o + 1) * columns] + ends_ref[i]
                copies.append(pltpu.make_async_copy(result.at[i], out_hbm.at[i], sent.at[i]))
                copies[-1].start()
        for copy in copies:
            copy.wait()

    vmem = pl.BlockSpec(memory_space=pltpu.VMEM)
    return pl.pallas_call(
        kernel,
        in_specs=[vmem] * 3,
        out_specs=pl.BlockSpec(memory_space=pltpu.HBM),
        out_shape=jax.ShapeDtypeStruct(ends.shape, F32),
        scratch_shapes=[pltpu.VMEM(ends.shape, F32), pltpu.SemaphoreType.DMA((groups * group,))],
        compiler_params=pltpu.CompilerParams(vmem_limit_bytes=8 * MIB),
        cost_estimate=costs(2.5e9),
    )(middle, wide, ends)


def across(a, b):
    return lax.dot_general(a, b, (((0,), (0,)), ((), ())), preferred_element_type=F32)


def gram_image(place, first, second, even_pair, odd_pair, swap, parts, sketch, scale):
    half, width = first.shape
    span, columns = sketch.shape
    tiles = len(parts)
    capacity = 2 * half // tiles
    places = lax.axis_size("tm")
    group = LANES // INPUTS
    pair = 2 * LANES
    groups = span // LANES

    def kernel(place_ref, first_ref, second_ref, even_ref, odd_ref, swap_ref, *refs):
        part_refs = refs[:tiles]
        sketch_ref, image_ref, own, left, right, lag, start, later, full, turned = refs[tiles:]
        spot = place_ref[0]
        odd = lax.rem(spot, 2)
        for m in range(tiles):
            at = slice(m * capacity, (m + 1) * capacity)
            source, base = (first_ref, 0) if m < tiles // 2 else (second_ref, half)
            keep = part_refs[m][capacity : capacity + TAIL, :][:1]
            own[at, :] = source[m * capacity - base : (m + 1) * capacity - base, :] * keep

        upper = lax.rem(spot // 2, 2)

        @pl.when(upper == 0)
        def _():
            left[2 * half : 3 * half, :] = odd_ref[...]
            right[3 * half :, :] = even_ref[...]

        @pl.when(upper == 1)
        def _():
            left[2 * half : 3 * half, :] = even_ref[...]
            right[3 * half :, :] = odd_ref[...]

        @pl.when(spot < 2)
        def _():
            left[2 * half : 3 * half, :] = jnp.zeros((half, width), BF16)

        @pl.when(spot >= places - 2)
        def _():
            right[3 * half :, :] = jnp.zeros((half, width), BF16)

        left[3 * half :, :] = own[half:, :]
        right[2 * half : 3 * half, :] = own[:half, :]

        @pl.when(odd == 0)
        def _():
            for m in range(tiles // 2, tiles):
                at = slice(m * capacity - half, (m + 1) * capacity - half)
                keep = part_refs[m][capacity : capacity + TAIL, :][:1]
                mine = swap_ref[at, :] * keep
                right[at, :] = mine
                left[half + m * capacity - half : half + (m + 1) * capacity - half, :] = mine
            left[:half, :] = own[half:, :]
            right[half : 2 * half, :] = right[3 * half :, :]

        @pl.when(odd == 1)
        def _():
            for m in range(tiles // 2):
                at = slice(m * capacity, (m + 1) * capacity)
                keep = part_refs[m][capacity : capacity + TAIL, :][:1]
                mine = swap_ref[at, :] * keep
                left[at, :] = mine
                right[half + m * capacity : half + (m + 1) * capacity, :] = mine
            right[:half, :] = own[:half, :]
            left[half : 2 * half, :] = left[2 * half : 3 * half, :]

        lag[...] = jnp.zeros_like(lag)

        for q in range(width // pair):
            at = slice(q * pair, (q + 1) * pair)
            low = q * pair
            same = across(own[:, at], own[:, low:])
            n = width - low
            lag[:, :n] += same[:LANES]
            lag[:, : n - LANES] += same[LANES:, LANES:]
            near = across(left[:half, at], right[:half, :])
            one = near + across(left[half : 2 * half, at], right[half : 2 * half, :])
            lag[:, n : n + width] += one[:LANES]
            lag[:, n - LANES : n - LANES + width] += one[LANES:]
            two = across(left[2 * half :, at], right[2 * half :, : low + pair])
            lag[:, n + width :] += two[:LANES, : low + LANES]
            lag[:, n + width - LANES :] += two[LANES:, :]

            start[at, low:width] = same
            start[at, width : 2 * width] = near

        strip = lag[:INPUTS, :span]
        for o in range(1, group):
            strip += pltpu.roll(lag[o * INPUTS : (o + 1) * INPUTS, :], span + LANES - o * INPUTS, 1)[:, :span]
        lane = lax.broadcasted_iota(jnp.int32, strip.shape, 1)
        strip = jnp.where(lane < INPUTS, 0.5 * strip, strip)
        for j in range(1, groups, 2):
            full[j * LANES : (j + 1) * LANES, (j - 1) * LANES : j * LANES] = jnp.zeros((LANES, LANES), F32)

        tile_lane = lax.broadcasted_iota(jnp.int32, (INPUTS, LANES), 1)
        half_first = jnp.where(tile_lane < INPUTS, 0.5, 1.0)
        steps_here = width // INPUTS

        def first_tile(value, change):
            if value.shape[1] == LANES:
                return change(value)
            return jnp.concatenate([change(value[:, :LANES]), value[:, LANES:]], axis=1)

        def place(step):
            return slice(step * INPUTS, (step + 1) * INPUTS), step // group * LANES, step % group * INPUTS

        def to_columns(steps):
            for step in steps:
                rows_of, first_lane, shift = place(step)
                if shift:
                    value = pltpu.roll(full[rows_of, first_lane:], shift, 1)
                    full[rows_of, first_lane:] = first_tile(
                        value, lambda tile: jnp.where(tile_lane < shift, 0.0, tile)
                    )

        def to_lags(last):
            for step in range(steps_here):
                rows_of, first_lane, shift = place(step)
                value = start[rows_of, first_lane:last]
                if shift:
                    value = pltpu.roll(value, value.shape[1] - shift, 1)
                start[rows_of, : last - first_lane] = first_tile(value, lambda tile: tile * half_first)

        @pl.when(spot >= 2)
        def _():
            for o in range(group):
                full[o * INPUTS : (o + 1) * INPUTS, :] = strip
            to_columns(range(group))
            for j in range(1, groups):
                full[j * LANES : (j + 1) * LANES, j * LANES :] = full[:LANES, : span - j * LANES]

        @pl.when(spot == 0)
        def _():
            to_lags(2 * width)
            rest = strip
            for step in range(steps_here):
                rows_of, first_lane, _ = place(step)
                rest = rest[:, : span - first_lane]
                full[rows_of, first_lane:] = rest
                rest -= start[rows_of, : 2 * width - first_lane]
            rest = rest[:, : span - width]
            for o in range(group):
                full[width + o * INPUTS : width + (o + 1) * INPUTS, width:] = rest
            to_columns(range(steps_here + group))
            source = slice(width, width + LANES)
            for j in range(width // LANES + 1, groups):
                full[j * LANES : (j + 1) * LANES, j * LANES :] = full[source, width : span + width - j * LANES]

        @pl.when(spot == 1)
        def _():
            blank = jnp.zeros((INPUTS, LANES), F32)
            for step in range(steps_here):
                rows_of, first_lane, shift = place(step)
                value = start[rows_of, width : 2 * width]
                if shift:
                    value = jnp.concatenate([blank, value], axis=1)
                    value = pltpu.roll(value, value.shape[1] - shift, 1)
                later[rows_of, : value.shape[1]] = value
            to_lags(width)
            rest = strip
            for step in range(steps_here):
                rows_of, first_lane, shift = place(step)
                rest = rest[:, : span - first_lane]
                full[rows_of, first_lane:] = rest
                length = width + (LANES if shift else 0)
                before = span - first_lane - length
                changed = rest[:, before:] - later[rows_of, :length]
                rest = jnp.concatenate([rest[:, :before], changed], axis=1) if before else changed
            rest = rest[:, : span - width]
            for step in range(steps_here):
                rows_of, first_lane, _ = place(step)
                rest = rest[:, : width - first_lane]
                full[width + step * INPUTS : width + (step + 1) * INPUTS, width + first_lane :] = rest
                rest -= start[rows_of, : width - first_lane]
            to_columns(range(2 * steps_here))

        for q in range(span // pair):
            at = slice(q * pair, (q + 1) * pair)
            value = full[at, q * pair :]
            high = value.astype(BF16)
            low = (value - high.astype(F32)).astype(BF16)
            below = sketch_ref[q * pair :, :]
            image_ref[at, :] = jnp.dot(high, below, preferred_element_type=F32) + jnp.dot(
                low, below, preferred_element_type=F32
            )
            tall = sketch_ref[at, :]
            down = across(tall, high) + across(tall, low)
            if q == 0:
                turned[...] = down
            else:
                turned[:, q * pair :] += down
        image_ref[...] = (image_ref[...] + turned[...].T) * scale

    vmem = pl.BlockSpec(memory_space=pltpu.VMEM)
    smem = pl.BlockSpec(memory_space=pltpu.SMEM)
    return pl.pallas_call(
        kernel,
        in_specs=[smem] + [vmem] * (6 + tiles),
        out_specs=vmem,
        out_shape=jax.ShapeDtypeStruct((span, columns), F32),
        scratch_shapes=[
            pltpu.VMEM((2 * half, width), BF16),
            pltpu.VMEM((4 * half, width), BF16),
            pltpu.VMEM((4 * half, width), BF16),
            pltpu.VMEM((LANES, span + LANES), F32),
            pltpu.VMEM((width, 2 * width), F32),
            pltpu.VMEM((width, width + LANES), F32),
            pltpu.VMEM((span, span), F32),
            pltpu.VMEM((columns, span), F32),
        ],
        compiler_params=pltpu.CompilerParams(vmem_limit_bytes=18 * MIB),
        cost_estimate=costs(5e9),
    )(place, first, second, even_pair, odd_pair, swap, *parts, sketch)


def reduce_scatter(total, axes, rounds, left=None, gate=None):
    count = math.prod(lax.axis_size(a) for a in axes)
    me = jnp.int32(0)
    for a in axes:
        me = me * lax.axis_size(a) + lax.axis_index(a)
    bits = int(math.log2(count))
    left = list(range(bits)) if left is None else left
    value = total
    if value.ndim == 2:
        value = total.reshape((2,) * bits + (total.shape[0] // count, total.shape[1]))
    for bunch in rounds:
        dims = [left.index(b) for b in bunch]
        value = jnp.moveaxis(value, dims, range(len(bunch)))
        rest = value.shape[len(bunch):]
        value = value.reshape((2 ** len(bunch),) + rest)
        mine = jnp.int32(0)
        for b in bunch:
            mine = mine * 2 + ((me >> (bits - 1 - b)) & 1)
        acc = lax.dynamic_index_in_dim(value, mine, 0, keepdims=False)
        came = []
        for mask in range(1, 2 ** len(bunch)):
            flip = 0
            for place, b in enumerate(bunch):
                if (mask >> (len(bunch) - 1 - place)) & 1:
                    flip |= 1 << (bits - 1 - b)
            piece = lax.dynamic_index_in_dim(value, mine ^ mask, 0, keepdims=False)
            if len(bunch) == 1:
                came.append(jnp.stack([crossed(part, axes, flip) for part in piece]))
            else:
                came.append(crossed(piece, axes, flip))
        if gate is not None and bunch is rounds[-1]:
            came, gate = lax.optimization_barrier((came, gate))
        for piece in came:
            acc = acc + piece
        value = acc
        for b in bunch:
            left.remove(b)
    return value if gate is None else (value, gate)


def local(state_tiles, sketch, probe_cell, probe_row):
    n_tiles = lax.axis_size("sensor")
    width = state_tiles.shape[1]
    steps_here = width // INPUTS
    *parts, wanted = pick_rows(state_tiles, probe_cell[0], probe_row[0])
    arrived = [parts[0]] + [crossed(parts[m], ("sensor",), m) for m in range(1, n_tiles)]
    first, second, swap, even_pair, odd_pair = prepare(parts)
    swapped = crossed(swap, ("tm",), 1)
    odd_pair = paired(odd_pair, 2, 1)
    even_pair = paired(even_pair, 2, 0)
    own_block = place_rows(wanted, arrived)
    own_block, first = lax.optimization_barrier((own_block, first))
    ahead = [paired(own_block, 2, odd) for odd in (0, 1)]
    scale = 1.0 / math.sqrt(SENS_DEV * n_tiles * steps_here * lax.axis_size("tm"))
    place = lax.axis_index("tm").astype(jnp.int32).reshape(1)
    total = gram_image(place, first, second, even_pair, odd_pair, swapped, arrived, sketch, scale)
    tm_bits = int(math.log2(lax.axis_size("tm")))
    sensor_bits = int(math.log2(n_tiles))
    last = tm_bits + sensor_bits - 1
    axes = ("tm", "sensor")
    total = reduce_scatter(total, axes, [[last]])
    total, ahead = lax.optimization_barrier((total, ahead))
    next_two = jnp.where(lax.rem(place[0] // 2, 2) == 0, ahead[0], ahead[1])
    next_two = jnp.where(place[0] < lax.axis_size("tm") - 2, next_two, 0)
    next_one = crossed(jnp.where(lax.rem(place[0], 2) == 0, next_two, own_block), ("tm",), 1)
    ends, wide = hankel_ends(own_block, next_two, sketch)
    left = list(range(last))
    total, ends = reduce_scatter(total, axes, [list(range(tm_bits - 1, last))], left, ends)
    hankel_sketch = hankel_middle(next_one, wide, ends)
    left = list(range(tm_bits - 1))
    column_image, hankel_sketch = reduce_scatter(total, axes, [left], list(left), hankel_sketch)
    return (hankel_sketch, column_image)


def solution(mesh):
    placed = (P("sensor", "tm"), P(), P("sensor", None, None), P("sensor", None, None))
    return jax.shard_map(
        local,
        mesh=mesh,
        in_specs=placed,
        out_specs=(P("tm", "sensor", None), P(("tm", "sensor"), None)),
        check_vma=False,
    )
```

```python
import math

import jax
import jax.numpy as jnp
from jax import lax
from jax.experimental import pallas as pl
from jax.experimental.pallas import tpu as pltpu
from jax.sharding import PartitionSpec as P

INPUTS = 16
SENS_DEV = 256
LANES = 128
TAIL = 16
MIB = 1024 * 1024
F32 = jnp.float32
BF16 = jnp.bfloat16


def costs(flops, bytes_accessed=0):
    return pl.CostEstimate(flops=int(flops), bytes_accessed=int(bytes_accessed), transcendentals=0)


def shifted(x, axis, by):
    count = lax.axis_size(axis)
    pairs = [(i, i + by) for i in range(count) if 0 <= i + by < count]
    return lax.ppermute(x, axis, pairs)


def paired(x, by, odd):
    count, width = lax.axis_size("tm"), lax.axis_size("sensor")
    low = [i for i in range(count - by) if (i // by) % 2 == odd]
    partner = {i: i + by for i in low} | {i + by: i for i in low}
    pairs = []
    for i in range(count):
        for j in range(width):
            target = partner[i] * width + j if i in partner else i * width + (j ^ 1)
            pairs.append((i * width + j, target))
    return lax.ppermute(x, ("tm", "sensor"), pairs)


def crossed(x, axes, mask):
    count = math.prod(lax.axis_size(a) for a in axes)
    return lax.ppermute(x, axes, [(i, i ^ mask) for i in range(count)])


def pick_rows(state_tiles, probe_cell, probe_row):
    cells_here, width = state_tiles.shape
    tiles, capacity = probe_cell.shape
    rows = tiles * capacity
    steps = 4
    chunk = cells_here // steps

    def kernel(cell_hbm, row_hbm, state_hbm, *refs):
        parts = refs[:tiles]
        row_ref, cell_ref, slot, total, state, came = refs[tiles:]
        me = lax.axis_index("sensor")
        copies = [pltpu.make_async_copy(cell_hbm, cell_ref, came.at[steps])]
        copies.append(pltpu.make_async_copy(row_hbm, row_ref, came.at[steps + 1]))
        for k in range(steps):
            at = slice(k * chunk, (k + 1) * chunk)
            copies.append(pltpu.make_async_copy(state_hbm.at[at, :], state.at[at, :], came.at[k]))
        for copy in copies:
            copy.start()
        copies[0].wait()
        copies[1].wait()
        for m in range(tiles):
            line = cell_ref[pl.ds(me ^ m, 1), :]
            slot[m * capacity : (m + 1) * capacity, :] = jnp.broadcast_to(line, (LANES, capacity)).T
        lane = lax.broadcasted_iota(jnp.int32, (rows, LANES), 1)
        wanted = slot[...]
        tile = (wanted // LANES).astype(F32).astype(BF16)
        within = jnp.where(lax.rem(wanted, LANES) == lane, 1.0, 0.0).astype(BF16)
        none = jnp.zeros_like(within)
        for k in range(steps):
            chosen = jnp.concatenate(
                [jnp.where(tile == jnp.asarray(c, BF16), within, none) for c in range(k * chunk // LANES, (k + 1) * chunk // LANES)],
                axis=1,
            )
            copies[2 + k].wait()
            got = jnp.dot(chosen, state[k * chunk : (k + 1) * chunk, :], preferred_element_type=F32)
            if k:
                got += total[...]
            if k < steps - 1:
                total[...] = got
        got = got.astype(BF16)
        for m in range(tiles):
            parts[m][:capacity, :] = got[m * capacity : (m + 1) * capacity]
            if m % 2 == 0:
                own, other = [
                    jnp.broadcast_to(jnp.where(row_ref[pl.ds(me ^ n, 1), :1] >= 0, 1.0, 0.0), (TAIL, width))
                    for n in (m, m + 1)
                ]
                upper_rows = lax.broadcasted_iota(jnp.int32, (TAIL, width), 0) < TAIL // 2
                parts[m][capacity:, :] = jnp.where(upper_rows, own, other).astype(BF16)

    shapes = [(capacity + (0 if m % 2 else TAIL), width) for m in range(tiles)]
    return pl.pallas_call(
        kernel,
        in_specs=[pl.BlockSpec(memory_space=pltpu.HBM)] * 3,
        out_specs=[pl.BlockSpec(memory_space=pltpu.VMEM)] * (tiles + 1),
        out_shape=[jax.ShapeDtypeStruct(s, BF16) for s in shapes] + [jax.ShapeDtypeStruct(probe_row.shape, jnp.int32)],
        scratch_shapes=[
            pltpu.VMEM(probe_cell.shape, jnp.int32),
            pltpu.VMEM((rows, LANES), jnp.int32),
            pltpu.VMEM((rows, width), F32),
            pltpu.VMEM((cells_here, width), BF16),
            pltpu.SemaphoreType.DMA((steps + 2,)),
        ],
        compiler_params=pltpu.CompilerParams(vmem_limit_bytes=10 * MIB),
        cost_estimate=costs(2 * rows * cells_here * width, 2 * cells_here * width),
    )(*[pltpu.with_memory_space_constraint(x, pltpu.HBM) for x in (probe_cell, probe_row, state_tiles)])


def place_rows(wanted, parts):
    tiles, capacity = wanted.shape
    width = parts[0].shape[1]

    def kernel(row_ref, *refs):
        out_ref = refs[tiles]
        me = lax.axis_index("sensor")
        sensor = lax.broadcasted_iota(jnp.int32, (SENS_DEV, capacity), 0)
        total = jnp.zeros((SENS_DEV, width), F32)
        for m in range(tiles):
            chosen = jnp.where(row_ref[pl.ds(me ^ m, 1), :] == sensor, 1.0, 0.0).astype(BF16)
            total += jnp.dot(chosen, refs[m][:capacity, :], preferred_element_type=F32)
        out_ref[...] = total.astype(BF16)

    return pl.pallas_call(
        kernel,
        out_shape=jax.ShapeDtypeStruct((SENS_DEV, width), BF16),
        compiler_params=pltpu.CompilerParams(vmem_limit_bytes=8 * MIB),
        cost_estimate=costs(2e10),
    )(wanted, *parts)


def prepare(parts):
    tiles = len(parts)
    capacity, width = parts[1].shape
    half = tiles * capacity // 2

    def kernel(*refs):
        first, second, swap, even_pair, odd_pair = refs[tiles:]
        spot = lax.axis_index("tm")
        odd = lax.rem(spot, 2)
        upper = lax.rem(spot // 2, 2)
        for m in range(tiles):
            base = 0 if m < tiles // 2 else half
            at = slice(m * capacity - base, (m + 1) * capacity - base)
            side = first if m < tiles // 2 else second
            side[at, :] = refs[m][:capacity, :]

        @pl.when(odd == 0)
        def _():
            swap[...] = first[...]

        @pl.when(odd == 1)
        def _():
            swap[...] = second[...]

        @pl.when(upper == 0)
        def _():
            even_pair[...] = first[...]
            odd_pair[...] = second[...]

        @pl.when(upper == 1)
        def _():
            even_pair[...] = second[...]
            odd_pair[...] = first[...]

    shapes = [(half, width)] * 5
    return pl.pallas_call(
        kernel,
        out_shape=[jax.ShapeDtypeStruct(s, BF16) for s in shapes],
        compiler_params=pltpu.CompilerParams(vmem_limit_bytes=8 * MIB),
        cost_estimate=costs(5e8),
    )(*parts)


def hankel_ends(first, last, sketch):
    rows, width = first.shape
    span, columns = sketch.shape
    group = LANES // INPUTS
    groups = width // LANES

    def kernel(first_ref, last_ref, sketch_ref, out_ref, wide):
        for o in range(group):
            at = slice(o * columns, (o + 1) * columns)
            top = o * INPUTS
            wide[top : top + span, at] = sketch_ref[...]
            if o:
                wide[:top, at] = jnp.zeros((top, columns), BF16)
            wide[top + span :, at] = jnp.zeros((LANES - top, columns), BF16)
        for g in range(groups):
            shift = g * LANES
            image = jnp.dot(first_ref[:, shift:], wide[: width - shift, :], preferred_element_type=F32)
            image += jnp.dot(last_ref[:, : shift + LANES], wide[span - shift :, :], preferred_element_type=F32)
            for o in range(group):
                out_ref[g * group + o] = image[:, o * columns : (o + 1) * columns]

    vmem = pl.BlockSpec(memory_space=pltpu.VMEM)
    return pl.pallas_call(
        kernel,
        in_specs=[vmem] * 3,
        out_specs=[vmem] * 2,
        out_shape=[
            jax.ShapeDtypeStruct((groups * group, rows, columns), F32),
            jax.ShapeDtypeStruct((span + LANES, group * columns), BF16),
        ],
        compiler_params=pltpu.CompilerParams(vmem_limit_bytes=8 * MIB),
        cost_estimate=costs(2.5e9),
    )(first, last, sketch)


def hankel_middle(middle, wide, ends):
    rows, width = middle.shape
    group = LANES // INPUTS
    groups = width // LANES
    columns = ends.shape[2]

    def kernel(middle_ref, wide_ref, ends_ref, out_hbm, result, sent):
        copies = []
        for g in range(groups):
            at = slice(width - g * LANES, 2 * width - g * LANES)
            image = jnp.dot(middle_ref[...], wide_ref[at, :], preferred_element_type=F32)
            for o in range(group):
                i = g * group + o
                result[i] = image[:, o * columns : (o + 1) * columns] + ends_ref[i]
                copies.append(pltpu.make_async_copy(result.at[i], out_hbm.at[i], sent.at[i]))
                copies[-1].start()
        for copy in copies:
            copy.wait()

    vmem = pl.BlockSpec(memory_space=pltpu.VMEM)
    return pl.pallas_call(
        kernel,
        in_specs=[vmem] * 3,
        out_specs=pl.BlockSpec(memory_space=pltpu.HBM),
        out_shape=jax.ShapeDtypeStruct(ends.shape, F32),
        scratch_shapes=[pltpu.VMEM(ends.shape, F32), pltpu.SemaphoreType.DMA((groups * group,))],
        compiler_params=pltpu.CompilerParams(vmem_limit_bytes=8 * MIB),
        cost_estimate=costs(2.5e9),
    )(middle, wide, ends)


def across(a, b):
    return lax.dot_general(a, b, (((0,), (0,)), ((), ())), preferred_element_type=F32)


def gram_image(place, first, second, even_pair, odd_pair, swap, marked, other, sketch, scale):
    half, width = first.shape
    span, columns = sketch.shape
    tiles = 2 * len(marked)
    capacity = 2 * half // tiles
    places = lax.axis_size("tm")
    group = LANES // INPUTS
    pair = 2 * LANES
    groups = span // LANES

    def kernel(place_ref, first_ref, second_ref, even_ref, odd_ref, swap_ref, *refs):
        mark_refs = refs[: tiles // 2]
        other_ref = refs[tiles // 2]
        sketch_ref, image_ref, own, left, right, lag, start, later, full, turned = refs[tiles // 2 + 1 :]
        spot = place_ref[0]
        odd = lax.rem(spot, 2)

        def mark_of(m):
            if m % 2 == 0:
                return mark_refs[m // 2][capacity : capacity + TAIL, :][:1]
            at = m // 2 * TAIL
            row = other_ref[at : at + TAIL, :][TAIL // 2 : TAIL // 2 + 1]
            return jnp.concatenate([row] * (width // LANES), axis=1)

        for m in range(tiles):
            at = slice(m * capacity, (m + 1) * capacity)
            source, base = (first_ref, 0) if m < tiles // 2 else (second_ref, half)
            keep = mark_of(m)
            own[at, :] = source[m * capacity - base : (m + 1) * capacity - base, :] * keep

        upper = lax.rem(spot // 2, 2)

        @pl.when(upper == 0)
        def _():
            left[2 * half : 3 * half, :] = odd_ref[...]
            right[3 * half :, :] = even_ref[...]

        @pl.when(upper == 1)
        def _():
            left[2 * half : 3 * half, :] = even_ref[...]
            right[3 * half :, :] = odd_ref[...]

        @pl.when(spot < 2)
        def _():
            left[2 * half : 3 * half, :] = jnp.zeros((half, width), BF16)

        @pl.when(spot >= places - 2)
        def _():
            right[3 * half :, :] = jnp.zeros((half, width), BF16)

        left[3 * half :, :] = own[half:, :]
        right[2 * half : 3 * half, :] = own[:half, :]

        @pl.when(odd == 0)
        def _():
            for m in range(tiles // 2, tiles):
                at = slice(m * capacity - half, (m + 1) * capacity - half)
                keep = mark_of(m)
                mine = swap_ref[at, :] * keep
                right[at, :] = mine
                left[half + m * capacity - half : half + (m + 1) * capacity - half, :] = mine
            left[:half, :] = own[half:, :]
            right[half : 2 * half, :] = right[3 * half :, :]

        @pl.when(odd == 1)
        def _():
            for m in range(tiles // 2):
                at = slice(m * capacity, (m + 1) * capacity)
                keep = mark_of(m)
                mine = swap_ref[at, :] * keep
                left[at, :] = mine
                right[half + m * capacity : half + (m + 1) * capacity, :] = mine
            right[:half, :] = own[:half, :]
            left[half : 2 * half, :] = left[2 * half : 3 * half, :]

        lag[...] = jnp.zeros_like(lag)

        for q in range(width // pair):
            at = slice(q * pair, (q + 1) * pair)
            low = q * pair
            same = across(own[:, at], own[:, low:])
            n = width - low
            lag[:, :n] += same[:LANES]
            lag[:, : n - LANES] += same[LANES:, LANES:]
            near = across(left[:half, at], right[:half, :])
            one = near + across(left[half : 2 * half, at], right[half : 2 * half, :])
            lag[:, n : n + width] += one[:LANES]
            lag[:, n - LANES : n - LANES + width] += one[LANES:]
            two = across(left[2 * half :, at], right[2 * half :, : low + pair])
            lag[:, n + width :] += two[:LANES, : low + LANES]
            lag[:, n + width - LANES :] += two[LANES:, :]

            start[at, low:width] = same
            start[at, width : 2 * width] = near

        strip = lag[:INPUTS, :span]
        for o in range(1, group):
            strip += pltpu.roll(lag[o * INPUTS : (o + 1) * INPUTS, :], span + LANES - o * INPUTS, 1)[:, :span]
        lane = lax.broadcasted_iota(jnp.int32, strip.shape, 1)
        strip = jnp.where(lane < INPUTS, 0.5 * strip, strip)
        for j in range(1, groups, 2):
            full[j * LANES : (j + 1) * LANES, (j - 1) * LANES : j * LANES] = jnp.zeros((LANES, LANES), F32)

        tile_lane = lax.broadcasted_iota(jnp.int32, (INPUTS, LANES), 1)
        half_first = jnp.where(tile_lane < INPUTS, 0.5, 1.0)
        steps_here = width // INPUTS

        def first_tile(value, change):
            if value.shape[1] == LANES:
                return change(value)
            return jnp.concatenate([change(value[:, :LANES]), value[:, LANES:]], axis=1)

        def place(step):
            return slice(step * INPUTS, (step + 1) * INPUTS), step // group * LANES, step % group * INPUTS

        def to_columns(steps):
            for step in steps:
                rows_of, first_lane, shift = place(step)
                if shift:
                    value = pltpu.roll(full[rows_of, first_lane:], shift, 1)
                    full[rows_of, first_lane:] = first_tile(
                        value, lambda tile: jnp.where(tile_lane < shift, 0.0, tile)
                    )

        def to_lags(last):
            for step in range(steps_here):
                rows_of, first_lane, shift = place(step)
                value = start[rows_of, first_lane:last]
                if shift:
                    value = pltpu.roll(value, value.shape[1] - shift, 1)
                start[rows_of, : last - first_lane] = first_tile(value, lambda tile: tile * half_first)

        @pl.when(spot >= 2)
        def _():
            for o in range(group):
                full[o * INPUTS : (o + 1) * INPUTS, :] = strip
            to_columns(range(group))
            for j in range(1, groups):
                full[j * LANES : (j + 1) * LANES, j * LANES :] = full[:LANES, : span - j * LANES]

        @pl.when(spot == 0)
        def _():
            to_lags(2 * width)
            rest = strip
            for step in range(steps_here):
                rows_of, first_lane, _ = place(step)
                rest = rest[:, : span - first_lane]
                full[rows_of, first_lane:] = rest
                rest -= start[rows_of, : 2 * width - first_lane]
            rest = rest[:, : span - width]
            for o in range(group):
                full[width + o * INPUTS : width + (o + 1) * INPUTS, width:] = rest
            to_columns(range(steps_here + group))
            source = slice(width, width + LANES)
            for j in range(width // LANES + 1, groups):
                full[j * LANES : (j + 1) * LANES, j * LANES :] = full[source, width : span + width - j * LANES]

        @pl.when(spot == 1)
        def _():
            blank = jnp.zeros((INPUTS, LANES), F32)
            for step in range(steps_here):
                rows_of, first_lane, shift = place(step)
                value = start[rows_of, width : 2 * width]
                if shift:
                    value = jnp.concatenate([blank, value], axis=1)
                    value = pltpu.roll(value, value.shape[1] - shift, 1)
                later[rows_of, : value.shape[1]] = value
            to_lags(width)
            rest = strip
            for step in range(steps_here):
                rows_of, first_lane, shift = place(step)
                rest = rest[:, : span - first_lane]
                full[rows_of, first_lane:] = rest
                length = width + (LANES if shift else 0)
                before = span - first_lane - length
                changed = rest[:, before:] - later[rows_of, :length]
                rest = jnp.concatenate([rest[:, :before], changed], axis=1) if before else changed
            rest = rest[:, : span - width]
            for step in range(steps_here):
                rows_of, first_lane, _ = place(step)
                rest = rest[:, : width - first_lane]
                full[width + step * INPUTS : width + (step + 1) * INPUTS, width + first_lane :] = rest
                rest -= start[rows_of, : width - first_lane]
            to_columns(range(2 * steps_here))

        for q in range(span // pair):
            at = slice(q * pair, (q + 1) * pair)
            value = full[at, q * pair :]
            high = value.astype(BF16)
            low = (value - high.astype(F32)).astype(BF16)
            below = sketch_ref[q * pair :, :]
            image_ref[at, :] = jnp.dot(high, below, preferred_element_type=F32) + jnp.dot(
                low, below, preferred_element_type=F32
            )
            tall = sketch_ref[at, :]
            down = across(tall, high) + across(tall, low)
            if q == 0:
                turned[...] = down
            else:
                turned[:, q * pair :] += down
        image_ref[...] = (image_ref[...] + turned[...].T) * scale

    vmem = pl.BlockSpec(memory_space=pltpu.VMEM)
    smem = pl.BlockSpec(memory_space=pltpu.SMEM)
    return pl.pallas_call(
        kernel,
        in_specs=[smem] + [vmem] * (7 + tiles // 2),
        out_specs=vmem,
        out_shape=jax.ShapeDtypeStruct((span, columns), F32),
        scratch_shapes=[
            pltpu.VMEM((2 * half, width), BF16),
            pltpu.VMEM((4 * half, width), BF16),
            pltpu.VMEM((4 * half, width), BF16),
            pltpu.VMEM((LANES, span + LANES), F32),
            pltpu.VMEM((width, 2 * width), F32),
            pltpu.VMEM((width, width + LANES), F32),
            pltpu.VMEM((span, span), F32),
            pltpu.VMEM((columns, span), F32),
        ],
        compiler_params=pltpu.CompilerParams(vmem_limit_bytes=18 * MIB),
        cost_estimate=costs(5e9),
    )(place, first, second, even_pair, odd_pair, swap, *marked, other, sketch)


def reduce_scatter(total, axes, rounds, left=None, gate=None):
    count = math.prod(lax.axis_size(a) for a in axes)
    me = jnp.int32(0)
    for a in axes:
        me = me * lax.axis_size(a) + lax.axis_index(a)
    bits = int(math.log2(count))
    left = list(range(bits)) if left is None else left
    value = total
    if value.ndim == 2:
        value = total.reshape((2,) * bits + (total.shape[0] // count, total.shape[1]))
    for bunch in rounds:
        dims = [left.index(b) for b in bunch]
        value = jnp.moveaxis(value, dims, range(len(bunch)))
        rest = value.shape[len(bunch):]
        value = value.reshape((2 ** len(bunch),) + rest)
        mine = jnp.int32(0)
        for b in bunch:
            mine = mine * 2 + ((me >> (bits - 1 - b)) & 1)
        acc = lax.dynamic_index_in_dim(value, mine, 0, keepdims=False)
        came = []
        for mask in range(1, 2 ** len(bunch)):
            flip = 0
            for place, b in enumerate(bunch):
                if (mask >> (len(bunch) - 1 - place)) & 1:
                    flip |= 1 << (bits - 1 - b)
            piece = lax.dynamic_index_in_dim(value, mine ^ mask, 0, keepdims=False)
            if len(bunch) == 1:
                came.append(jnp.stack([crossed(part, axes, flip) for part in piece]))
            else:
                came.append(crossed(piece, axes, flip))
        if gate is not None and bunch is rounds[-1]:
            came, gate = lax.optimization_barrier((came, gate))
        for piece in came:
            acc = acc + piece
        value = acc
        for b in bunch:
            left.remove(b)
    return value if gate is None else (value, gate)


def local(state_tiles, sketch, probe_cell, probe_row):
    n_tiles = lax.axis_size("sensor")
    width = state_tiles.shape[1]
    steps_here = width // INPUTS
    *parts, wanted = pick_rows(state_tiles, probe_cell[0], probe_row[0])
    arrived = [parts[0]] + [crossed(parts[m], ("sensor",), m) for m in range(1, n_tiles)]
    first, second, swap, even_pair, odd_pair = prepare(parts)
    swapped = crossed(swap, ("tm",), 1)
    odd_pair = paired(odd_pair, 2, 1)
    even_pair = paired(even_pair, 2, 0)
    marked = arrived[::2]
    other = jnp.concatenate([part[-TAIL:, :LANES] for part in marked])
    other = crossed(other, ("sensor",), 1)
    own_block = place_rows(wanted, arrived)
    own_block, first = lax.optimization_barrier((own_block, first))
    ahead = [paired(own_block, 2, odd) for odd in (0, 1)]
    scale = 1.0 / math.sqrt(SENS_DEV * n_tiles * steps_here * lax.axis_size("tm"))
    place = lax.axis_index("tm").astype(jnp.int32).reshape(1)
    total = gram_image(place, first, second, even_pair, odd_pair, swapped, marked, other, sketch, scale)
    tm_bits = int(math.log2(lax.axis_size("tm")))
    sensor_bits = int(math.log2(n_tiles))
    last = tm_bits + sensor_bits - 1
    axes = ("tm", "sensor")
    total = reduce_scatter(total, axes, [[last]])
    total, ahead = lax.optimization_barrier((total, ahead))
    next_two = jnp.where(lax.rem(place[0] // 2, 2) == 0, ahead[0], ahead[1])
    next_two = jnp.where(place[0] < lax.axis_size("tm") - 2, next_two, 0)
    next_one = crossed(jnp.where(lax.rem(place[0], 2) == 0, next_two, own_block), ("tm",), 1)
    ends, wide = hankel_ends(own_block, next_two, sketch)
    left = list(range(last))
    total, ends = reduce_scatter(total, axes, [list(range(tm_bits - 1, last))], left, ends)
    hankel_sketch = hankel_middle(next_one, wide, ends)
    left = list(range(tm_bits - 1))
    column_image, hankel_sketch = reduce_scatter(total, axes, [left], list(left), hankel_sketch)
    return (hankel_sketch, column_image)


def solution(mesh):
    placed = (P("sensor", "tm"), P(), P("sensor", None, None), P("sensor", None, None))
    return jax.shard_map(
        local,
        mesh=mesh,
        in_specs=placed,
        out_specs=(P("tm", "sensor", None), P(("tm", "sensor"), None)),
        check_vma=False,
    )
```

```python
import math

import jax
import jax.numpy as jnp
from jax import lax
from jax.experimental import pallas as pl
from jax.experimental.pallas import tpu as pltpu
from jax.sharding import PartitionSpec as P

INPUTS = 16
SENS_DEV = 256
LANES = 128
TAIL = 16
MIB = 1024 * 1024
F32 = jnp.float32
BF16 = jnp.bfloat16


def costs(flops, bytes_accessed=0):
    return pl.CostEstimate(flops=int(flops), bytes_accessed=int(bytes_accessed), transcendentals=0)


def shifted(x, axis, by):
    count = lax.axis_size(axis)
    pairs = [(i, i + by) for i in range(count) if 0 <= i + by < count]
    return lax.ppermute(x, axis, pairs)


def paired(x, by, odd):
    count, width = lax.axis_size("tm"), lax.axis_size("sensor")
    low = [i for i in range(count - by) if (i // by) % 2 == odd]
    partner = {i: i + by for i in low} | {i + by: i for i in low}
    pairs = []
    for i in range(count):
        for j in range(width):
            target = partner[i] * width + j if i in partner else i * width + (j ^ 1)
            pairs.append((i * width + j, target))
    return lax.ppermute(x, ("tm", "sensor"), pairs)


def crossed(x, axes, mask):
    count = math.prod(lax.axis_size(a) for a in axes)
    return lax.ppermute(x, axes, [(i, i ^ mask) for i in range(count)])


def pick_rows(state_tiles, probe_cell, probe_row):
    cells_here, width = state_tiles.shape
    tiles, capacity = probe_cell.shape
    rows = tiles * capacity
    steps = 4
    chunk = cells_here // steps

    def kernel(cell_hbm, row_hbm, state_hbm, *refs):
        parts = refs[:tiles]
        row_ref, cell_ref, slot, total, state, came = refs[tiles:]
        me = lax.axis_index("sensor")
        copies = [pltpu.make_async_copy(cell_hbm, cell_ref, came.at[steps])]
        copies.append(pltpu.make_async_copy(row_hbm, row_ref, came.at[steps + 1]))
        for k in range(steps):
            at = slice(k * chunk, (k + 1) * chunk)
            copies.append(pltpu.make_async_copy(state_hbm.at[at, :], state.at[at, :], came.at[k]))
        for copy in copies:
            copy.start()
        copies[0].wait()
        copies[1].wait()
        for m in range(tiles):
            line = cell_ref[pl.ds(me ^ m, 1), :]
            slot[m * capacity : (m + 1) * capacity, :] = jnp.broadcast_to(line, (LANES, capacity)).T
        lane = lax.broadcasted_iota(jnp.int32, (rows, LANES), 1)
        wanted = slot[...]
        tile = (wanted // LANES).astype(F32).astype(BF16)
        within = jnp.where(lax.rem(wanted, LANES) == lane, 1.0, 0.0).astype(BF16)
        none = jnp.zeros_like(within)
        for k in range(steps):
            chosen = jnp.concatenate(
                [jnp.where(tile == jnp.asarray(c, BF16), within, none) for c in range(k * chunk // LANES, (k + 1) * chunk // LANES)],
                axis=1,
            )
            copies[2 + k].wait()
            got = jnp.dot(chosen, state[k * chunk : (k + 1) * chunk, :], preferred_element_type=F32)
            if k:
                got += total[...]
            if k < steps - 1:
                total[...] = got
        got = got.astype(BF16)
        for m in range(tiles):
            parts[m][:capacity, :] = got[m * capacity : (m + 1) * capacity]
            if m % 2 == 0:
                own, other = [
                    jnp.broadcast_to(jnp.where(row_ref[pl.ds(me ^ n, 1), :1] >= 0, 1.0, 0.0), (TAIL, width))
                    for n in (m, m + 1)
                ]
                upper_rows = lax.broadcasted_iota(jnp.int32, (TAIL, width), 0) < TAIL // 2
                parts[m][capacity:, :] = jnp.where(upper_rows, own, other).astype(BF16)

    shapes = [(capacity + (0 if m % 2 else TAIL), width) for m in range(tiles)]
    return pl.pallas_call(
        kernel,
        in_specs=[pl.BlockSpec(memory_space=pltpu.HBM)] * 3,
        out_specs=[pl.BlockSpec(memory_space=pltpu.VMEM)] * (tiles + 1),
        out_shape=[jax.ShapeDtypeStruct(s, BF16) for s in shapes] + [jax.ShapeDtypeStruct(probe_row.shape, jnp.int32)],
        scratch_shapes=[
            pltpu.VMEM(probe_cell.shape, jnp.int32),
            pltpu.VMEM((rows, LANES), jnp.int32),
            pltpu.VMEM((rows, width), F32),
            pltpu.VMEM((cells_here, width), BF16),
            pltpu.SemaphoreType.DMA((steps + 2,)),
        ],
        compiler_params=pltpu.CompilerParams(vmem_limit_bytes=10 * MIB),
        cost_estimate=costs(2 * rows * cells_here * width, 2 * cells_here * width),
    )(*[pltpu.with_memory_space_constraint(x, pltpu.HBM) for x in (probe_cell, probe_row, state_tiles)])


def place_rows(wanted, parts):
    tiles, capacity = wanted.shape
    width = parts[0].shape[1]

    def kernel(row_ref, *refs):
        out_ref = refs[tiles]
        me = lax.axis_index("sensor")
        sensor = lax.broadcasted_iota(jnp.int32, (SENS_DEV, capacity), 0)
        total = jnp.zeros((SENS_DEV, width), F32)
        for m in range(tiles):
            chosen = jnp.where(row_ref[pl.ds(me ^ m, 1), :] == sensor, 1.0, 0.0).astype(BF16)
            total += jnp.dot(chosen, refs[m][:capacity, :], preferred_element_type=F32)
        out_ref[...] = total.astype(BF16)

    return pl.pallas_call(
        kernel,
        out_shape=jax.ShapeDtypeStruct((SENS_DEV, width), BF16),
        compiler_params=pltpu.CompilerParams(vmem_limit_bytes=8 * MIB),
        cost_estimate=costs(2e10),
    )(wanted, *parts)


def prepare(parts):
    tiles = len(parts)
    capacity, width = parts[1].shape
    half = tiles * capacity // 2

    def kernel(*refs):
        first, second, swap, even_pair, odd_pair = refs[tiles:]
        spot = lax.axis_index("tm")
        odd = lax.rem(spot, 2)
        upper = lax.rem(spot // 2, 2)
        for m in range(tiles):
            base = 0 if m < tiles // 2 else half
            at = slice(m * capacity - base, (m + 1) * capacity - base)
            side = first if m < tiles // 2 else second
            side[at, :] = refs[m][:capacity, :]

        @pl.when(odd == 0)
        def _():
            swap[...] = first[...]

        @pl.when(odd == 1)
        def _():
            swap[...] = second[...]

        @pl.when(upper == 0)
        def _():
            even_pair[...] = first[...]
            odd_pair[...] = second[...]

        @pl.when(upper == 1)
        def _():
            even_pair[...] = second[...]
            odd_pair[...] = first[...]

    shapes = [(half, width)] * 5
    return pl.pallas_call(
        kernel,
        out_shape=[jax.ShapeDtypeStruct(s, BF16) for s in shapes],
        compiler_params=pltpu.CompilerParams(vmem_limit_bytes=8 * MIB),
        cost_estimate=costs(5e8),
    )(*parts)


def hankel_ends(first, last, sketch):
    rows, width = first.shape
    span, columns = sketch.shape
    group = LANES // INPUTS
    groups = width // LANES

    def kernel(first_ref, last_ref, sketch_ref, out_ref, wide):
        for o in range(group):
            at = slice(o * columns, (o + 1) * columns)
            top = o * INPUTS
            wide[top : top + span, at] = sketch_ref[...]
            if o:
                wide[:top, at] = jnp.zeros((top, columns), BF16)
            wide[top + span :, at] = jnp.zeros((LANES - top, columns), BF16)
        for g in range(groups):
            shift = g * LANES
            image = jnp.dot(first_ref[:, shift:], wide[: width - shift, :], preferred_element_type=F32)
            image += jnp.dot(last_ref[:, : shift + LANES], wide[span - shift :, :], preferred_element_type=F32)
            for o in range(group):
                out_ref[g * group + o] = image[:, o * columns : (o + 1) * columns]

    vmem = pl.BlockSpec(memory_space=pltpu.VMEM)
    return pl.pallas_call(
        kernel,
        in_specs=[vmem] * 3,
        out_specs=[vmem] * 2,
        out_shape=[
            jax.ShapeDtypeStruct((groups * group, rows, columns), F32),
            jax.ShapeDtypeStruct((span + LANES, group * columns), BF16),
        ],
        compiler_params=pltpu.CompilerParams(vmem_limit_bytes=8 * MIB),
        cost_estimate=costs(2.5e9),
    )(first, last, sketch)


def hankel_middle(middle, wide, ends):
    rows, width = middle.shape
    group = LANES // INPUTS
    groups = width // LANES
    columns = ends.shape[2]

    def kernel(middle_ref, wide_ref, ends_ref, out_hbm, result, sent):
        copies = []
        for g in range(groups):
            at = slice(width - g * LANES, 2 * width - g * LANES)
            image = jnp.dot(middle_ref[...], wide_ref[at, :], preferred_element_type=F32)
            for o in range(group):
                i = g * group + o
                result[i] = image[:, o * columns : (o + 1) * columns] + ends_ref[i]
                copies.append(pltpu.make_async_copy(result.at[i], out_hbm.at[i], sent.at[i]))
                copies[-1].start()
        for copy in copies:
            copy.wait()

    vmem = pl.BlockSpec(memory_space=pltpu.VMEM)
    return pl.pallas_call(
        kernel,
        in_specs=[vmem] * 3,
        out_specs=pl.BlockSpec(memory_space=pltpu.HBM),
        out_shape=jax.ShapeDtypeStruct(ends.shape, F32),
        scratch_shapes=[pltpu.VMEM(ends.shape, F32), pltpu.SemaphoreType.DMA((groups * group,))],
        compiler_params=pltpu.CompilerParams(vmem_limit_bytes=8 * MIB),
        cost_estimate=costs(2.5e9),
    )(middle, wide, ends)


def across(a, b):
    return lax.dot_general(a, b, (((0,), (0,)), ((), ())), preferred_element_type=F32)


def gram_image(place, first, second, even_pair, odd_pair, swap, marked, other, sketch, scale):
    half, width = first.shape
    span, columns = sketch.shape
    tiles = 2 * len(marked)
    capacity = 2 * half // tiles
    places = lax.axis_size("tm")
    group = LANES // INPUTS
    pair = 2 * LANES
    groups = span // LANES

    def kernel(place_ref, first_ref, second_ref, even_ref, odd_ref, swap_ref, *refs):
        mark_refs = refs[: tiles // 2]
        other_ref = refs[tiles // 2]
        sketch_ref, image_ref, own, left, right, lag, start, later, full, turned = refs[tiles // 2 + 1 :]
        spot = place_ref[0]
        odd = lax.rem(spot, 2)

        def mark_of(m):
            if m % 2 == 0:
                return mark_refs[m // 2][capacity : capacity + TAIL, :][:1]
            at = m // 2 * TAIL
            row = other_ref[at : at + TAIL, :][TAIL // 2 : TAIL // 2 + 1]
            return jnp.concatenate([row] * (width // LANES), axis=1)

        for m in range(tiles):
            at = slice(m * capacity, (m + 1) * capacity)
            source, base = (first_ref, 0) if m < tiles // 2 else (second_ref, half)
            keep = mark_of(m)
            own[at, :] = source[m * capacity - base : (m + 1) * capacity - base, :] * keep

        upper = lax.rem(spot // 2, 2)

        @pl.when(upper == 0)
        def _():
            left[2 * half : 3 * half, :] = odd_ref[...]
            right[3 * half :, :] = even_ref[...]

        @pl.when(upper == 1)
        def _():
            left[2 * half : 3 * half, :] = even_ref[...]
            right[3 * half :, :] = odd_ref[...]

        @pl.when(spot < 2)
        def _():
            left[2 * half : 3 * half, :] = jnp.zeros((half, width), BF16)

        @pl.when(spot >= places - 2)
        def _():
            right[3 * half :, :] = jnp.zeros((half, width), BF16)

        left[3 * half :, :] = own[half:, :]
        right[2 * half : 3 * half, :] = own[:half, :]

        @pl.when(odd == 0)
        def _():
            for m in range(tiles // 2, tiles):
                at = slice(m * capacity - half, (m + 1) * capacity - half)
                keep = mark_of(m)
                mine = swap_ref[at, :] * keep
                right[at, :] = mine
                left[half + m * capacity - half : half + (m + 1) * capacity - half, :] = mine
            left[:half, :] = own[half:, :]
            right[half : 2 * half, :] = right[3 * half :, :]

        @pl.when(odd == 1)
        def _():
            for m in range(tiles // 2):
                at = slice(m * capacity, (m + 1) * capacity)
                keep = mark_of(m)
                mine = swap_ref[at, :] * keep
                left[at, :] = mine
                right[half + m * capacity : half + (m + 1) * capacity, :] = mine
            right[:half, :] = own[:half, :]
            left[half : 2 * half, :] = left[2 * half : 3 * half, :]

        lag[...] = jnp.zeros_like(lag)

        for q in range(width // pair):
            at = slice(q * pair, (q + 1) * pair)
            low = q * pair
            same = across(own[:, at], own[:, low:])
            n = width - low
            lag[:, :n] += same[:LANES]
            lag[:, : n - LANES] += same[LANES:, LANES:]
            near = across(left[:half, at], right[:half, :])
            one = near + across(left[half : 2 * half, at], right[half : 2 * half, :])
            lag[:, n : n + width] += one[:LANES]
            lag[:, n - LANES : n - LANES + width] += one[LANES:]
            two = across(left[2 * half :, at], right[2 * half :, : low + pair])
            lag[:, n + width :] += two[:LANES, : low + LANES]
            lag[:, n + width - LANES :] += two[LANES:, :]

            start[at, low:width] = same
            start[at, width : 2 * width] = near

        strip = lag[:INPUTS, :span]
        for o in range(1, group):
            strip += pltpu.roll(lag[o * INPUTS : (o + 1) * INPUTS, :], span + LANES - o * INPUTS, 1)[:, :span]
        lane = lax.broadcasted_iota(jnp.int32, strip.shape, 1)
        strip = jnp.where(lane < INPUTS, 0.5 * strip, strip)
        for j in range(1, groups, 2):
            full[j * LANES : (j + 1) * LANES, (j - 1) * LANES : j * LANES] = jnp.zeros((LANES, LANES), F32)

        tile_lane = lax.broadcasted_iota(jnp.int32, (INPUTS, LANES), 1)
        half_first = jnp.where(tile_lane < INPUTS, 0.5, 1.0)
        steps_here = width // INPUTS

        def first_tile(value, change):
            if value.shape[1] == LANES:
                return change(value)
            return jnp.concatenate([change(value[:, :LANES]), value[:, LANES:]], axis=1)

        def place(step):
            return slice(step * INPUTS, (step + 1) * INPUTS), step // group * LANES, step % group * INPUTS

        def to_columns(steps):
            for step in steps:
                rows_of, first_lane, shift = place(step)
                if shift:
                    value = pltpu.roll(full[rows_of, first_lane:], shift, 1)
                    full[rows_of, first_lane:] = first_tile(
                        value, lambda tile: jnp.where(tile_lane < shift, 0.0, tile)
                    )

        def to_lags(last):
            for step in range(steps_here):
                rows_of, first_lane, shift = place(step)
                value = start[rows_of, first_lane:last]
                if shift:
                    value = pltpu.roll(value, value.shape[1] - shift, 1)
                start[rows_of, : last - first_lane] = first_tile(value, lambda tile: tile * half_first)

        @pl.when(spot >= 2)
        def _():
            for o in range(group):
                full[o * INPUTS : (o + 1) * INPUTS, :] = strip
            to_columns(range(group))
            for j in range(1, groups):
                full[j * LANES : (j + 1) * LANES, j * LANES :] = full[:LANES, : span - j * LANES]

        @pl.when(spot == 0)
        def _():
            to_lags(2 * width)
            rest = strip
            for step in range(steps_here):
                rows_of, first_lane, _ = place(step)
                rest = rest[:, : span - first_lane]
                full[rows_of, first_lane:] = rest
                rest -= start[rows_of, : 2 * width - first_lane]
            rest = rest[:, : span - width]
            for o in range(group):
                full[width + o * INPUTS : width + (o + 1) * INPUTS, width:] = rest
            to_columns(range(steps_here + group))
            source = slice(width, width + LANES)
            for j in range(width // LANES + 1, groups):
                full[j * LANES : (j + 1) * LANES, j * LANES :] = full[source, width : span + width - j * LANES]

        @pl.when(spot == 1)
        def _():
            blank = jnp.zeros((INPUTS, LANES), F32)
            for step in range(steps_here):
                rows_of, first_lane, shift = place(step)
                value = start[rows_of, width : 2 * width]
                if shift:
                    value = jnp.concatenate([blank, value], axis=1)
                    value = pltpu.roll(value, value.shape[1] - shift, 1)
                later[rows_of, : value.shape[1]] = value
            to_lags(width)
            rest = strip
            for step in range(steps_here):
                rows_of, first_lane, shift = place(step)
                rest = rest[:, : span - first_lane]
                full[rows_of, first_lane:] = rest
                length = width + (LANES if shift else 0)
                before = span - first_lane - length
                changed = rest[:, before:] - later[rows_of, :length]
                rest = jnp.concatenate([rest[:, :before], changed], axis=1) if before else changed
            rest = rest[:, : span - width]
            for step in range(steps_here):
                rows_of, first_lane, _ = place(step)
                rest = rest[:, : width - first_lane]
                full[width + step * INPUTS : width + (step + 1) * INPUTS, width + first_lane :] = rest
                rest -= start[rows_of, : width - first_lane]
            to_columns(range(2 * steps_here))

        for q in range(span // pair):
            at = slice(q * pair, (q + 1) * pair)
            value = full[at, q * pair :]
            high = value.astype(BF16)
            low = (value - high.astype(F32)).astype(BF16)
            below = sketch_ref[q * pair :, :]
            image_ref[at, :] = jnp.dot(high, below, preferred_element_type=F32) + jnp.dot(
                low, below, preferred_element_type=F32
            )
            tall = sketch_ref[at, :]
            down = across(tall, high) + across(tall, low)
            if q == 0:
                turned[...] = down
            else:
                turned[:, q * pair :] += down
        image_ref[...] = (image_ref[...] + turned[...].T) * scale

    vmem = pl.BlockSpec(memory_space=pltpu.VMEM)
    smem = pl.BlockSpec(memory_space=pltpu.SMEM)
    return pl.pallas_call(
        kernel,
        in_specs=[smem] + [vmem] * (7 + tiles // 2),
        out_specs=vmem,
        out_shape=jax.ShapeDtypeStruct((span, columns), F32),
        scratch_shapes=[
            pltpu.VMEM((2 * half, width), BF16),
            pltpu.VMEM((4 * half, width), BF16),
            pltpu.VMEM((4 * half, width), BF16),
            pltpu.VMEM((LANES, span + LANES), F32),
            pltpu.VMEM((width, 2 * width), F32),
            pltpu.VMEM((width, width + LANES), F32),
            pltpu.VMEM((span, span), F32),
            pltpu.VMEM((columns, span), F32),
        ],
        compiler_params=pltpu.CompilerParams(vmem_limit_bytes=18 * MIB),
        cost_estimate=costs(5e9),
    )(place, first, second, even_pair, odd_pair, swap, *marked, other, sketch)


def reduce_scatter(total, axes, rounds, left=None, gate=None):
    count = math.prod(lax.axis_size(a) for a in axes)
    me = jnp.int32(0)
    for a in axes:
        me = me * lax.axis_size(a) + lax.axis_index(a)
    bits = int(math.log2(count))
    left = list(range(bits)) if left is None else left
    value = total
    if value.ndim == 2:
        value = total.reshape((2,) * bits + (total.shape[0] // count, total.shape[1]))
    for bunch in rounds:
        dims = [left.index(b) for b in bunch]
        value = jnp.moveaxis(value, dims, range(len(bunch)))
        rest = value.shape[len(bunch):]
        value = value.reshape((2 ** len(bunch),) + rest)
        mine = jnp.int32(0)
        for b in bunch:
            mine = mine * 2 + ((me >> (bits - 1 - b)) & 1)
        acc = lax.dynamic_index_in_dim(value, mine, 0, keepdims=False)
        came = []
        for mask in range(1, 2 ** len(bunch)):
            flip = 0
            for place, b in enumerate(bunch):
                if (mask >> (len(bunch) - 1 - place)) & 1:
                    flip |= 1 << (bits - 1 - b)
            piece = lax.dynamic_index_in_dim(value, mine ^ mask, 0, keepdims=False)
            if len(bunch) == 1:
                came.append(jnp.stack([crossed(part, axes, flip) for part in piece]))
            else:
                came.append(crossed(piece, axes, flip))
        if gate is not None and bunch is rounds[-1]:
            came, gate = lax.optimization_barrier((came, gate))
        for piece in came:
            acc = acc + piece
        value = acc
        for b in bunch:
            left.remove(b)
    return value if gate is None else (value, gate)


def local(state_tiles, sketch, probe_cell, probe_row):
    n_tiles = lax.axis_size("sensor")
    width = state_tiles.shape[1]
    steps_here = width // INPUTS
    *parts, wanted = pick_rows(state_tiles, probe_cell[0], probe_row[0])
    arrived = [parts[0]] + [crossed(parts[m], ("sensor",), m) for m in range(1, n_tiles)]
    first, second, swap, even_pair, odd_pair = prepare(parts)
    swap, arrived[1] = lax.optimization_barrier((swap, arrived[1]))
    swapped = crossed(swap, ("tm",), 1)
    odd_pair = paired(odd_pair, 2, 1)
    even_pair = paired(even_pair, 2, 0)
    marked = arrived[::2]
    other = jnp.concatenate([part[-TAIL:, :LANES] for part in marked])
    other = crossed(other, ("sensor",), 1)
    own_block = place_rows(wanted, arrived)
    own_block, first = lax.optimization_barrier((own_block, first))
    ahead = [paired(own_block, 2, odd) for odd in (1, 0)]
    scale = 1.0 / math.sqrt(SENS_DEV * n_tiles * steps_here * lax.axis_size("tm"))
    place = lax.axis_index("tm").astype(jnp.int32).reshape(1)
    total = gram_image(place, first, second, even_pair, odd_pair, swapped, marked, other, sketch, scale)
    tm_bits = int(math.log2(lax.axis_size("tm")))
    sensor_bits = int(math.log2(n_tiles))
    last = tm_bits + sensor_bits - 1
    axes = ("tm", "sensor")
    total = reduce_scatter(total, axes, [[last]])
    total, ahead = lax.optimization_barrier((total, ahead))
    next_two = jnp.where(lax.rem(place[0] // 2, 2) == 0, ahead[1], ahead[0])
    next_two = jnp.where(place[0] < lax.axis_size("tm") - 2, next_two, 0)
    next_one = crossed(jnp.where(lax.rem(place[0], 2) == 0, next_two, own_block), ("tm",), 1)
    ends, wide = hankel_ends(own_block, next_two, sketch)
    left = list(range(last))
    total, ends = reduce_scatter(total, axes, [list(range(tm_bits - 1, last))], left, ends)
    hankel_sketch = hankel_middle(next_one, wide, ends)
    left = list(range(tm_bits - 1))
    column_image, hankel_sketch = reduce_scatter(total, axes, [left], list(left), hankel_sketch)
    return (hankel_sketch, column_image)


def solution(mesh):
    placed = (P("sensor", "tm"), P(), P("sensor", None, None), P("sensor", None, None))
    return jax.shard_map(
        local,
        mesh=mesh,
        in_specs=placed,
        out_specs=(P("tm", "sensor", None), P(("tm", "sensor"), None)),
        check_vma=False,
    )
```
